32 devices in a mesh: band: 4 (over x, core), dom: 8 (over z, y).
Axes of the slice: x: 2, y: 2, z: 4, core: 2. Of those that a mesh axis runs over, the one named last changes fastest.
Arguments:
- occupied: float32 [256, 12288], P('band', 'dom'), may hold values from -6 to 6
- start_guess: float32 [1, 256, 12288], P(None, 'band', 'dom'), may hold values from -0.6 to 0.6
- potential: float32 [12288], P('dom'), may hold values from 0.5 to 8
- perturbation: float32 [1, 12288], P(None, 'dom'), may hold values from -6 to 6
- band_energy: float32 [256], P('band'), may hold values from -4 to -0.5
- beta_radial: float32 [512], replicated, may hold values from -0.25 to 0.25
- beta_slope: float32 [512], replicated, may hold values from -0.25 to 0.25
- atom_owner: int32 [32], replicated, may hold values from 0 to 7, as said below
- atom_site: int32 [3, 32], replicated, may hold values from 0 to 15, as said below
- sphere_offset: int32 [3, 512], replicated, may hold values from -5 to 5
- displaced: int32 [1], replicated, may hold values from 0 to 31
Outputs:
- solution: float32 [1, 256, 12288], P(None, 'band', 'dom')
- residual: float32 [1, 256, 12288], P(None, 'band', 'dom')
The draws below stay inside these ranges and needn't reach their ends.
Inputs may be any that keep to these rules, and one draw needn't show every extreme that they name: `atom_owner`: each slab owns at most 8 atoms and some slab owns exactly 8. `atom_site`: row 0 lies below 6, row 1 below 16, row 2 below 16. Atom 0 sits on plane 5 of its slab, row 15 and column 15; atom 1 on plane 0, row 0 and column 0.
All inputs are finite; a program needn't handle non-finite values.
Results may differ from the reference program's by a relative error of at most 0.0003.
Values sent between devices are 32-bit elements; how exact they have to be, the bound alone decides.
A program may use at most 128 MiB of HBM per device.

```python
import math
import jax
import jax.numpy as jnp
from jax import lax

NOCC = 256
NPERT = 1
CZ = 6
NY = 16
NX = 16
ITERS = 2
RAD = 5
PTS = 512
NZ = 48
NCELLS = 12288
NATOM = 32
MOST = 8


def draw_atom_owner(key, part):
    base_key = jax.random.fold_in(key, 11)
    slab_total = NZ // CZ
    busiest = jax.random.randint(jax.random.fold_in(base_key, 1), (), 0, slab_total).astype(jnp.int32)
    slots = jax.random.permutation(jax.random.fold_in(base_key, 2), (slab_total - 1) * MOST)[:NATOM - MOST]
    others = (slots // MOST).astype(jnp.int32)
    others = others + (others >= busiest).astype(jnp.int32)
    owners = jnp.concatenate([jnp.zeros((MOST,), jnp.int32) + busiest, others])
    return jax.random.permutation(jax.random.fold_in(base_key, 3), owners).astype(jnp.int32)


def draw_atom_site(key, part):
    base_key = jax.random.fold_in(key, 23)
    planes = jax.random.randint(jax.random.fold_in(base_key, 1), (NATOM,), 0, CZ)
    row_index = jax.random.randint(jax.random.fold_in(base_key, 2), (NATOM,), 0, NY)
    column_index = jax.random.randint(jax.random.fold_in(base_key, 3), (NATOM,), 0, NX)
    planes = planes.at[0].set(CZ - 1).at[1].set(0)
    row_index = row_index.at[0].set(NY - 1).at[1].set(0)
    column_index = column_index.at[0].set(NX - 1).at[1].set(0)
    return jnp.stack([planes, row_index, column_index]).astype(jnp.int32)


def draw_sphere_offset(key, part):
    base_key = jax.random.fold_in(key, 37)
    offsets = jax.random.randint(base_key, (3, PTS), -RAD, RAD + 1).astype(jnp.int32)
    offsets = offsets.at[0, 0].set(-RAD)
    offsets = offsets.at[0, 1].set(RAD)
    return offsets.astype(jnp.int32)


def shard_levels(own_key, dims, cuts, smallest, high):
    def one(axis_at, blocks):
        draws = jax.random.uniform(jax.random.fold_in(jax.random.fold_in(own_key, 6), axis_at), (blocks,), jnp.float32, smallest / len(cuts), high / len(cuts))
        return jnp.repeat(jnp.exp(draws), dims[axis_at] // blocks).reshape((-1,) + (1,) * (len(dims) - axis_at - 1))

    factor_of = one(*cuts[0])
    for cut in cuts[1:]:
        factor_of = factor_of * one(*cut)
    return factor_of


def centred(key, extent, scale, reach, pieces=(), held_as=jnp.bfloat16):
    factor_of = shard_levels(key, extent, pieces, -0.22, 0.18) if pieces else 1.0
    entries = jax.random.normal(key, extent, jnp.float32) * scale * factor_of
    return jnp.minimum(jnp.maximum(entries, -reach), reach).astype(held_as)


def setup_inputs(seed: int = 0) -> dict:
    streams_of = jax.random.split(jax.random.key(seed), 12)
    return {
        "occupied": centred(streams_of[0], (NOCC, NCELLS), 1.0, 6.0, ((0, 4), (1, 8)), jnp.float32),
        "start_guess": centred(streams_of[1], (NPERT, NOCC, NCELLS), 0.1, 0.6, ((1, 4), (2, 8)), jnp.float32),
        "potential": jnp.clip(jnp.exp(math.log(8.0) - 2.7725887 * jax.random.uniform(streams_of[2], (NCELLS,), jnp.float32) ** shard_levels(streams_of[2], (NCELLS,), ((0, 8),), -0.2, 0.2)), 0.5, 8.0),
        "perturbation": centred(streams_of[3], (NPERT, NCELLS), 1.0, 6.0, ((1, 8),), jnp.float32),
        "band_energy": jnp.clip(-4.0 + 3.5 * jax.random.uniform(streams_of[4], (NOCC,), jnp.float32) ** shard_levels(streams_of[4], (NOCC,), ((0, 4),), -0.2, 0.2), -4.0, -0.5),
        "beta_radial": centred(streams_of[5], (PTS,), PTS ** -0.5, 0.25, (), jnp.float32),
        "beta_slope": centred(streams_of[6], (PTS,), PTS ** -0.5, 0.25, (), jnp.float32),
        "atom_owner": draw_atom_owner(jax.random.fold_in(streams_of[11], 71), 0),
        "atom_site": draw_atom_site(jax.random.fold_in(streams_of[11], 71), 0),
        "sphere_offset": draw_sphere_offset(jax.random.fold_in(streams_of[11], 71), 0),
        "displaced": jax.random.randint(streams_of[10], (NPERT,), 0, NATOM).astype(jnp.int32),
    }


COEF = (-5369.0 / 1800.0, 12.0 / 7.0, -15.0 / 56.0, 10.0 / 189.0, -1.0 / 112.0, 2.0 / 825.0, -1.0 / 1386.0)
KINETIC = 2.0
SHIFT = 20.0
STRENGTH = 10.0
HIGH = lax.Precision.HIGHEST


def kinetic_part(field):
    grid = field.reshape(NPERT, NOCC, NZ, NY, NX)
    total = 3.0 * COEF[0] * grid
    for axis_number in (2, 3, 4):
        for distance in range(1, len(COEF)):
            total = total + COEF[distance] * (jnp.roll(grid, distance, axis_number) + jnp.roll(grid, -distance, axis_number))
    return (-KINETIC * total).reshape(field.shape)


def point_index(atom_owner, atom_site, sphere_offset):
    planes = ((atom_owner * CZ + atom_site[0])[:, None] + sphere_offset[0][None, :]) % NZ
    row_index = (atom_site[1][:, None] + sphere_offset[1][None, :]) % NY
    column_index = (atom_site[2][:, None] + sphere_offset[2][None, :]) % NX
    return ((planes * NY + row_index) * NX + column_index).astype(jnp.int32)


def nonlocal_part(field, point_cell, beta_radial):
    def per_layer(layer_field):
        values = layer_field[:, point_cell]
        projection = jnp.einsum("bak,k->ba", values, beta_radial, precision=HIGH)
        update = STRENGTH * projection[:, :, None] * beta_radial[None, None, :]
        return jnp.zeros_like(layer_field).at[:, point_cell].add(update)
    return lax.map(per_layer, field)


def occupied_part(field, occupied):
    flat_field = field.reshape(-1, NCELLS)
    correlation = jnp.dot(occupied, flat_field.T, precision=HIGH, preferred_element_type=jnp.float32)
    back = jnp.dot(correlation.T, occupied, precision=HIGH, preferred_element_type=jnp.float32)
    return (back / NCELLS).reshape(field.shape)


def reference(occupied, start_guess, potential, perturbation, band_energy, beta_radial, beta_slope, atom_owner, atom_site, sphere_offset, displaced):
    point_cell = point_index(atom_owner, atom_site, sphere_offset)

    def operator(field):
        onsite = (potential[None, None, :] - band_energy[None, :, None]) * field
        return kinetic_part(field) + onsite + nonlocal_part(field, point_cell, beta_radial) + SHIFT * occupied_part(field, occupied)

    disp_cells = point_cell[displaced]
    values = occupied[:, disp_cells]
    first_proj = jnp.einsum("npk,k->pn", values, beta_radial, precision=HIGH)
    second_proj = jnp.einsum("npk,k->pn", values, beta_slope, precision=HIGH)
    update = STRENGTH * (first_proj[:, :, None] * beta_slope[None, None, :] + second_proj[:, :, None] * beta_radial[None, None, :])
    mixed = perturbation[:, None, :] * occupied[None, :, :]
    pert_ids = jnp.arange(NPERT, dtype=jnp.int32)[:, None, None]
    band_ids = jnp.arange(NOCC, dtype=jnp.int32)[None, :, None]
    mixed = mixed.at[pert_ids, band_ids, disp_cells[:, None, :]].add(update)
    rhs = -(mixed - occupied_part(mixed, occupied))

    solution = start_guess
    residual = rhs - operator(start_guess)
    direction = residual
    norm_now = jnp.sum(residual * residual, axis=2)
    for iteration in range(ITERS):
        image = operator(direction)
        alpha = norm_now / jnp.sum(direction * image, axis=2)
        solution = solution + alpha[:, :, None] * direction
        residual = residual - alpha[:, :, None] * image
        if iteration + 1 < ITERS:
            norm_next = jnp.sum(residual * residual, axis=2)
            direction = residual + (norm_next / norm_now)[:, :, None] * direction
            norm_now = norm_next
    return solution, residual
```

```python
import functools
import numpy as np
import jax
import jax.numpy as jnp
from jax import lax
from jax.experimental import pallas as pl
from jax.experimental.pallas import tpu as pltpu
from jax.sharding import PartitionSpec as P

NY = 16
NX = 16
PLANE = NY * NX
HALO = 6
CHUNKS = 8
SUM_AT = 3
FINISH = 4
RAD = 5

COEF = (
    -5369.0 / 1800.0,
    12.0 / 7.0,
    -15.0 / 56.0,
    10.0 / 189.0,
    -1.0 / 112.0,
    2.0 / 825.0,
    -1.0 / 1386.0,
)
KINETIC = 2.0
SHIFT = 20.0
STRENGTH = 10.0
HIGH = lax.Precision.HIGHEST


def plane_matrix():
    full = np.zeros((PLANE, PLANE), np.float64)
    for y in range(NY):
        for x in range(NX):
            at = y * NX + x
            full[at, at] += 3.0 * COEF[0]
            for d in range(1, 7):
                for s in (d, -d):
                    full[((y + s) % NY) * NX + x, at] += COEF[d]
                    full[y * NX + (x + s) % NX, at] += COEF[d]
    return (-KINETIC * full).astype(np.float32)


def fields_kernel(slabs, depth, radial, slope, offset, owner, site, displaced, out, padded):
    atoms = owner.shape[0]
    planes = slabs * depth
    points = offset.shape[1]
    slab = lax.axis_index("dom")
    rows = lax.broadcasted_iota(jnp.int32, (16, points), 0)
    along_z = rows == offset[0:1, :] + RAD
    in_plane = (offset[1:2, :] & (NY - 1)) * NX + (offset[2:3, :] & (NX - 1))
    hot = jnp.where(
        lax.broadcasted_iota(jnp.int32, (PLANE, points), 0) == in_plane, 1.0, 0.0
    ).astype(jnp.float32)
    left = jnp.concatenate(
        [jnp.where(along_z, radial[...], 0.0), jnp.where(along_z, slope[...], 0.0)], axis=0
    )
    template = lax.dot_general(
        left, hot, (((1,), (1,)), ((), ())), precision=HIGH, preferred_element_type=jnp.float32
    )
    padded[...] = jnp.zeros_like(padded)
    for which in range(2):
        part = template[16 * which : 16 * which + 16]
        padded[which, 0:16, :] = part
        padded[which, planes : planes + 16, :] = part
    column = lax.broadcasted_iota(jnp.int32, (8, PLANE), 1) & (NX - 1)

    def shifted(which, a):
        z = lax.rem(slab * depth + RAD + 2 * planes - owner[a] * depth - site[0, a], planes)
        x = site[2, a]
        turn = site[1, a] * NX + x
        start = pl.multiple_of(lax.div(z, 8) * 8, 8)
        block = pltpu.roll(padded[which, pl.ds(start, 16), :], lax.rem(16 - lax.rem(z, 8), 16), 0)[0:8]
        first = pltpu.roll(block, turn, 1)
        second = pltpu.roll(block, lax.rem(turn + PLANE - NX, PLANE), 1)
        return jnp.where(column >= x, first, second)

    out[atoms:, :] = jnp.zeros((out.shape[0] - atoms, out.shape[1]), jnp.float32)
    for row in range(atoms + 2):
        field = shifted(0, row) if row < atoms else shifted(row - atoms, displaced[0])
        for z in range(depth):
            out[row : row + 1, z * PLANE : (z + 1) * PLANE] = field[z : z + 1]


def place_fields(slab, slabs, depth, atoms, radial, slope, offset, owner, site, displaced, fields):
    planes = slabs * depth
    points = offset.shape[1]
    count = atoms + 8
    rows = lax.broadcasted_iota(jnp.int32, (16, points), 0)
    along_z = rows == offset[0:1, :] + RAD
    in_plane = (offset[1:2, :] & (NY - 1)) * NX + (offset[2:3, :] & (NX - 1))
    hot = jnp.where(
        lax.broadcasted_iota(jnp.int32, (PLANE, points), 0) == in_plane, 1.0, 0.0
    ).astype(jnp.float32)
    left = jnp.concatenate(
        [jnp.where(along_z, radial[...], 0.0), jnp.where(along_z, slope[...], 0.0)], axis=0
    )
    template = lax.dot_general(
        left, hot, (((1,), (1,)), ((), ())), precision=HIGH, preferred_element_type=jnp.float32
    )
    row = lax.broadcasted_iota(jnp.int32, (count, atoms), 0)
    atom = lax.broadcasted_iota(jnp.int32, (count, atoms), 1)
    chosen = atom == jnp.where(row < atoms, row, displaced[0])

    def column(values):
        return jnp.sum(jnp.where(chosen, values, 0), axis=1, keepdims=True)

    centre = column(owner[...]) * depth + column(site[0:1, :])
    turn_y, turn_x = column(site[1:2, :]), column(site[2:3, :])
    row = lax.broadcasted_iota(jnp.int32, (count, 32), 0)
    lane = lax.broadcasted_iota(jnp.int32, (count, 32), 1)
    picks = []
    for z in range(depth):
        at = slab * depth + (z + RAD) - centre
        at = jnp.where(at < 0, at + planes, jnp.where(at >= planes, at - planes, at))
        at = jnp.where(at < 16, at, -32)
        pick = lane == at + jnp.where(row == atoms + 1, 16, 0)
        picks.append(jnp.where(pick & (row < atoms + 2), 1.0, 0.0).astype(jnp.float32))
    value = lax.dot_general(
        jnp.concatenate(picks, axis=0),
        template,
        (((1,), (0,)), ((), ())),
        precision=HIGH,
        preferred_element_type=jnp.float32,
    )
    x = lax.broadcasted_iota(jnp.int32, (count, PLANE), 1) & (NX - 1)
    wide_x = jnp.broadcast_to(turn_x, (count, PLANE))
    wide_y = jnp.broadcast_to(turn_y, (count, PLANE))
    fields[atoms:, :] = jnp.zeros((fields.shape[0] - atoms, fields.shape[1]), jnp.float32)
    for z in range(depth):
        block = value[z * count : (z + 1) * count]
        for d in (1, 2, 4, 8):
            near, far = pltpu.roll(block, d, 1), pltpu.roll(block, PLANE + d - NX, 1)
            block = jnp.where((wide_x & d) != 0, jnp.where(x >= d, near, far), block)
        for d in (1, 2, 4, 8):
            block = jnp.where((wide_y & d) != 0, pltpu.roll(block, d * NX, 1), block)
        fields[0:count, z * PLANE : (z + 1) * PLANE] = block


def atom_fields(slabs, cells, beta_radial, beta_slope, offset, owner, site, displaced):
    atoms = owner.shape[0]
    depth = cells // PLANE
    vmem = pl.BlockSpec(memory_space=pltpu.VMEM)
    smem = pl.BlockSpec(memory_space=pltpu.SMEM)
    return pl.pallas_call(
        functools.partial(fields_kernel, slabs, depth),
        out_shape=jax.ShapeDtypeStruct((max(128, atoms + 16), cells), jnp.float32),
        in_specs=[vmem, vmem, vmem, smem, smem, smem],
        out_specs=vmem,
        scratch_shapes=[pltpu.VMEM((2, slabs * depth + 16, PLANE), jnp.float32)],
        compiler_params=pltpu.CompilerParams(vmem_limit_bytes=16 * 1024 * 1024),
    )(beta_radial[None, :], beta_slope[None, :], offset, owner, site, displaced)


def times(a, b, dims):
    return lax.dot_general(a, b, (dims, ((), ())), precision=HIGH, preferred_element_type=jnp.float32)


def plain(occupied, start, potential, perturbation, energy, beta, pair, in_plane):
    slabs = lax.axis_size("dom")
    bands, cells = start.shape
    depth = cells // PLANE
    total = cells * slabs
    whole = lax.all_gather(occupied, "band", axis=0, tiled=True)
    every = whole.shape[0]
    up = [(i, (i + 1) % slabs) for i in range(slabs)]
    down = [(j, i) for i, j in up]

    def local_part(field):
        before = lax.ppermute(field, "dom", up)
        after = lax.ppermute(field, "dom", down)
        grid = jnp.concatenate([before, field, after], axis=1)
        image = times(field.reshape(bands * depth, PLANE), in_plane, ((1,), (0,))).reshape(bands, cells)
        for d in range(1, 7):
            low = (depth - d) * PLANE
            high = (depth + d) * PLANE
            image += (-KINETIC * COEF[d]) * (grid[:, low : low + cells] + grid[:, high : high + cells])
        return image + (potential - energy) * field

    def correlate(field):
        return jnp.concatenate(
            [times(field, whole, ((1,), (1,))), times(field, beta, ((1,), (1,)))], axis=1
        )

    def operator(field, total_correlation):
        return (
            local_part(field)
            + (SHIFT / total) * times(total_correlation[:, :every], whole, ((1,), (0,)))
            + STRENGTH * times(total_correlation[:, every:], beta, ((1,), (0,)))
        )

    def dot(u, v):
        return jnp.sum(u * v, axis=1, keepdims=True)

    shaped = perturbation * occupied
    first, on_atoms, own, of_all = lax.psum(
        (
            times(shaped - SHIFT * start, whole, ((1,), (1,))),
            times(start, beta, ((1,), (1,))),
            times(occupied, pair, ((1,), (1,))),
            times(pair, whole, ((1,), (1,))),
        ),
        "dom",
    )
    own_radial, own_slope = own[:, 0:1], own[:, 1:2]
    first = first + STRENGTH * (own_radial * of_all[1:2] + own_slope * of_all[0:1])
    residual = (
        times(first * (1.0 / total), whole, ((1,), (0,)))
        - STRENGTH * times(on_atoms, beta, ((1,), (0,)))
        - local_part(start)
        - shaped
        - STRENGTH * (own_radial * pair[1:2] + own_slope * pair[0:1])
    )
    correlation, norm = lax.psum((correlate(residual), dot(residual, residual)), "dom")
    image = operator(residual, correlation)
    correlation, curve = lax.psum((correlate(image), dot(residual, image)), "dom")
    alpha = norm / curve
    again = operator(image, correlation)
    later = residual - alpha * image
    later_image = image - alpha * again
    new, bend, cross = lax.psum((dot(later, later), dot(later, later_image), dot(later, image)), "dom")
    ratio = new / norm
    step = new / (bend + ratio * (2.0 * cross + ratio * curve))
    answer = start + alpha * residual + step * (later + ratio * residual)
    return answer, later - step * (later_image + ratio * image)


NT = (((1,), (1,)), ((), ()))
NN = (((1,), (0,)), ((), ()))
MESH = pl.DeviceIdType.MESH


def parts_of(x):
    high = x.astype(jnp.bfloat16)
    return high, (x - high.astype(jnp.float32)).astype(jnp.bfloat16)


def product(a, b, dims):
    def one(u, v):
        return lax.dot_general(u, v, dims, preferred_element_type=jnp.float32)

    return one(a[0], b[0]) + (one(a[0], b[1]) + one(a[1], b[0]))


def fused_kernel(
    atoms,
    slabs,
    occ_in,
    start_in,
    pot_in,
    pert_in,
    energy_in,
    radial_in,
    slope_in,
    offset_in,
    owner_in,
    site_in,
    displaced,
    start,
    r0,
    w0,
    image,
    weights,
    occ,
    pot,
    pert,
    energy_row,
    radial,
    slope,
    offset,
    owner,
    site,
    energy,
    fields,
    plane_high,
    plane_low,
    whole,
    w_high,
    w_low,
    f_high,
    f_low,
    faces,
    part,
    pieces,
    summed,
    totals,
    rows_part,
    rows_in,
    last_part,
    last_in,
    band_send,
    band_recv,
    face_send,
    face_recv,
    hand_send,
    hand_recv,
    sum_send,
    sum_recv,
    all_send,
    all_recv,
    rows_send,
    rows_recv,
    last_send,
    last_recv,
    local_sem,
):
    bands, cells = occ.shape
    every = 4 * bands
    total = cells * slabs
    band = lax.axis_index("band")
    slab = lax.axis_index("dom")
    sibling = band + 1 - 2 * (band % 2)
    across = (band + 2) % 4
    barrier = pltpu.get_barrier_semaphore()
    pl.semaphore_signal(barrier, inc=1, device_id={"band": sibling}, device_id_type=MESH)
    pl.semaphore_signal(barrier, inc=1, device_id={"band": across}, device_id_type=MESH)
    peers = [(slab + k) % slabs for k in range(slabs)]
    for k in range(1, slabs):
        pl.semaphore_signal(barrier, inc=1, device_id={"dom": peers[k]}, device_id_type=MESH)
    loads = [
        pltpu.make_async_copy(src, dst, local_sem.at[i])
        for i, (src, dst) in enumerate(
            (
                (offset_in, offset),
                (radial_in, radial),
                (slope_in, slope),
                (owner_in, owner),
                (site_in, site),
                (energy_in, energy_row),
                (pot_in, pot),
                (pert_in, pert),
                (start_in, start),
                (occ_in, occ),
            )
        )
    ]
    for load in loads:
        load.start()
    pl.semaphore_wait(barrier, slabs + 1)

    pending = []

    def send(src, dst, send_sem, recv_sem, device):
        copy = pltpu.make_async_remote_copy(
            src_ref=src,
            dst_ref=dst,
            send_sem=send_sem,
            recv_sem=recv_sem,
            device_id=device,
            device_id_type=MESH,
        )
        copy.start()
        pending.append(copy)
        return copy

    chunk = bands // CHUNKS
    side = slab % 2
    beside = slab + 1 - 2 * side
    beyond = (slab + slabs + 2 - 4 * side) % slabs

    def send_face(turn, field, c):
        return send(
            field.at[pl.ds(c * chunk, chunk)],
            faces.at[turn, side, pl.ds(c * chunk, chunk)],
            face_send.at[turn, c],
            face_recv.at[turn, c],
            {"dom": beside},
        )

    def hand_over(turn, c):
        return send(
            faces.at[turn, 1 - side, pl.ds(c * chunk, chunk)],
            faces.at[turn, side, pl.ds(c * chunk, chunk)],
            hand_send.at[turn, c],
            hand_recv.at[turn, c],
            {"dom": beyond},
        )

    def hand_on(turn, copies, c):
        copies[c].wait_recv()
        copies.append(hand_over(turn, c))

    half = bands // 2
    crossing = [
        send(
            occ_in.at[pl.ds(c * half, half)],
            whole.at[1, pl.ds(c * half, half)],
            band_send.at[c],
            band_recv.at[c],
            {"band": across},
        )
        for c in range(2)
    ]
    to_sibling = send(occ_in, whole.at[0], band_send.at[2], band_recv.at[2], {"band": sibling})
    moving = [send_face(0, start_in, c) for c in range(CHUNKS)]

    def hold(row, block):
        high, low = parts_of(block)
        w_high[row : row + block.shape[0], :] = high
        w_low[row : row + block.shape[0], :] = low

    def hold_field(block):
        high, low = parts_of(block)
        f_high[...] = high
        f_low[...] = low

    def plane_image(field, planes):
        for z in planes:
            cut = slice(z * PLANE, (z + 1) * PLANE)
            local_pot = jnp.concatenate(
                [pot[i : i + 1] for i in range(z * PLANE // 128, (z + 1) * PLANE // 128)], axis=1
            )
            image[:, cut] = product(
                (f_high[:, cut], f_low[:, cut]), (plane_high[...], plane_low[...]), NN
            ) + (local_pot - energy[:, 0:1]) * field[:, cut]

    def across_planes(turn, field, c):
        def group(i, carry):
            rows = pl.ds(pl.multiple_of(i * 8, 8), 8)
            grid = [
                ref[rows, z * PLANE : (z + 1) * PLANE]
                for ref in (faces.at[turn, 0], field, faces.at[turn, 1])
                for z in range(HALO)
            ]
            for z in range(HALO):
                cut = slice(z * PLANE, (z + 1) * PLANE)
                value = image[rows, cut]
                for d in range(1, 7):
                    value += (-KINETIC * COEF[d]) * (grid[HALO + z - d] + grid[HALO + z + d])
                image[rows, cut] = value
            return carry

        lax.fori_loop(c * chunk // 8, (c + 1) * chunk // 8, group, 0)

    def start_sum(turn):
        return [
            send(
                part.at[turn, pl.ds(pl.multiple_of(peers[k] * 8, 8), 8)],
                pieces.at[turn, k],
                sum_send.at[turn, k],
                sum_recv.at[turn, k],
                {"dom": peers[k]},
            )
            for k in range(1, slabs)
        ]

    def share_sum(turn, copies):
        mine = pl.ds(pl.multiple_of(slab * 8, 8), 8)
        value = part[turn, mine, :]
        for k in range(1, slabs):
            copies[k - 1].wait_recv()
            value += pieces[turn, k]
        summed[turn] = value
        shared = [
            send(
                summed.at[turn],
                totals.at[turn, mine],
                all_send.at[turn, k],
                all_recv.at[turn, k],
                {"dom": peers[k]},
            )
            for k in range(1, slabs)
        ]
        totals[turn, mine, :] = value
        return shared

    def finish_sum(shared):
        for copy in shared:
            copy.wait_recv()

    lane = lax.broadcasted_iota(jnp.int32, (bands, 128), 1)

    def correlate(rows):
        return product((f_high[...], f_low[...]), (w_high[rows, :], w_low[rows, :]), NT)

    def back(coefficients):
        return product(parts_of(coefficients), (w_high[...], w_low[...]), NN)

    one_cell = lax.broadcasted_iota(jnp.int32, (PLANE, PLANE), 0)
    other_cell = lax.broadcasted_iota(jnp.int32, (PLANE, PLANE), 1)
    along_x = (one_cell - other_cell) & (NX - 1)
    along_y = ((one_cell >> 4) - (other_cell >> 4)) & (NY - 1)
    away_x = jnp.minimum(along_x, NX - along_x)
    away_y = jnp.minimum(along_y, NY - along_y)
    away = jnp.where(away_x == 0, away_y, jnp.where(away_y == 0, away_x, NX))
    matrix = jnp.where(away == 0, -KINETIC * 3.0 * COEF[0], 0.0)
    for d in range(1, 7):
        matrix = jnp.where(away == d, -KINETIC * COEF[d], matrix)
    matrix_high, matrix_low = parts_of(matrix.astype(jnp.float32))
    plane_high[...] = matrix_high
    plane_low[...] = matrix_low

    for load in loads[:8]:
        load.wait()
    rows = lax.broadcasted_iota(jnp.int32, (bands, bands), 0)
    columns = lax.broadcasted_iota(jnp.int32, (bands, bands), 1)
    energy[...] = jnp.broadcast_to(
        jnp.sum(jnp.where(rows == columns, energy_row[...], 0.0), axis=1, keepdims=True), (bands, 128)
    )
    place_fields(
        slab, slabs, cells // PLANE, atoms, radial, slope, offset, owner, site, displaced, fields
    )
    for load in loads[8:]:
        load.wait()
    hold(0, occ[...])
    hold(every, fields[...])
    hold_field(start[...])
    plane_image(start, range(HALO))
    hand_on(0, moving, 0)
    hand_on(0, moving, 1)
    ends = slice(every, every + 128)
    on_start = correlate(ends)
    on_own = product(
        (w_high[0:bands, :], w_low[0:bands, :]), (w_high[ends, :], w_low[ends, :]), NT
    )
    part[0, :, every:] = jnp.where(lane < atoms, on_start, on_own)
    hand_on(0, moving, 2)
    shaped = pert[...] * occ[...]
    hold_field(shaped - SHIFT * start[...])
    to_sibling.wait_recv()
    hold(bands, whole[0])
    hand_on(0, moving, 3)
    part[0, :, 0 : 2 * bands] = correlate(slice(0, 2 * bands))
    passed = []
    for c in range(2):
        crossing[c].wait_recv()
        passed.append(
            send(
                whole.at[1, pl.ds(c * half, half)],
                whole.at[2, pl.ds(c * half, half)],
                band_send.at[3 + c],
                band_recv.at[3 + c],
                {"band": sibling},
            )
        )
        hand_on(0, moving, 4 + 2 * c)
        hand_on(0, moving, 5 + 2 * c)
    hold(2 * bands, whole[1])
    for copy in passed:
        copy.wait_recv()
    hold(3 * bands, whole[2])
    part[0, :, 2 * bands : every] = correlate(slice(2 * bands, every))
    copies = start_sum(0)
    pair = slice(every + atoms, every + atoms + 16)
    rows_part[...] = product(
        (w_high[pair, :], w_low[pair, :]), (w_high[0:every, :], w_low[0:every, :]), NT
    )[0:8]
    row_copies = [
        send(rows_part, rows_in.at[k], rows_send.at[k], rows_recv.at[k], {"dom": peers[k]})
        for k in range(1, slabs)
    ]
    shared = share_sum(0, copies)
    for c in range(CHUNKS):
        moving[CHUNKS + c].wait_recv()
        across_planes(0, start, c)
    of_all = rows_part[...]
    for k in range(1, slabs):
        row_copies[k - 1].wait_recv()
        of_all += rows_in[k]
    finish_sum(shared)
    last = totals[0, :, every:]
    own_radial, own_slope = last[:, atoms : atoms + 1], last[:, atoms + 1 : atoms + 2]
    first = totals[0, :, 0:every] + STRENGTH * (own_radial * of_all[1:2] + own_slope * of_all[0:1])
    ends_part = jnp.where(
        lane < atoms,
        last,
        jnp.where(lane == atoms, own_slope, jnp.where(lane == atoms + 1, own_radial, 0.0)),
    )
    r0[...] = (
        back(jnp.concatenate([first * (1.0 / total), -STRENGTH * ends_part], axis=1))
        - image[...]
        - pert[...] * occ[...]
    )

    def apply(turn, field, scalar):
        face = [send_face(turn, field, c) for c in range(2)]
        hold_field(field[...])
        part[turn, :, 0:every] = correlate(slice(0, every))
        part[turn, :, every:] = jnp.where(lane == atoms, scalar, correlate(ends))
        copies = start_sum(turn)
        face += [send_face(turn, field, c) for c in range(2, CHUNKS)]
        plane_image(field, range(HALO))
        handed = []
        for c in range(CHUNKS):
            face[c].wait_recv()
            handed.append(hand_over(turn, c))
            if c == SUM_AT:
                shared = share_sum(turn, copies)
            if c >= 4:
                handed[c - 4].wait_recv()
                across_planes(turn, field, c - 4)
        finish_sum(shared)
        last = totals[turn, :, every:]
        coefficients = jnp.concatenate(
            [
                totals[turn, :, 0:every] * (SHIFT / total),
                jnp.where(lane < atoms, STRENGTH * last, 0.0),
            ],
            axis=1,
        )
        image[...] += back(coefficients)
        for c in range(CHUNKS - 4, CHUNKS):
            handed[c].wait_recv()
            across_planes(turn, field, c)
        return last[:, atoms : atoms + 1]

    def dot(u, v):
        return jnp.sum(u * v, axis=1, keepdims=True)

    norm = apply(1, r0, dot(r0[...], r0[...]))
    w0[...] = image[...]
    curve = apply(2, w0, dot(r0[...], w0[...]))
    alpha = norm / curve
    later = r0[...] - alpha * w0[...]
    later_image = w0[...] - alpha * image[...]
    three = jnp.where(
        lane == 0,
        dot(later, later),
        jnp.where(
            lane == 1, dot(later, later_image), jnp.where(lane == 2, dot(later, w0[...]), 0.0)
        ),
    )
    eye = jnp.where(
        lax.broadcasted_iota(jnp.int32, (128, 128), 0)
        == lax.broadcasted_iota(jnp.int32, (128, 128), 1),
        1.0,
        0.0,
    ).astype(jnp.float32)
    three = jnp.concatenate([three, jnp.zeros((128 - bands, 128), jnp.float32)], axis=0)
    last_part[...] = lax.dot_general(
        eye[0:8], three, NT, precision=HIGH, preferred_element_type=jnp.float32
    )
    last_copies = [
        send(last_part, last_in.at[k], last_send.at[k], last_recv.at[k], {"dom": peers[k]})
        for k in range(1, slabs)
    ]
    value = last_part[...]
    for k in range(1, slabs):
        last_copies[k - 1].wait_recv()
        value += last_in[k]
    three = lax.dot_general(
        eye[0:bands], value, NT, precision=HIGH, preferred_element_type=jnp.float32
    )
    new, bend, cross = three[:, 0:1], three[:, 1:2], three[:, 2:3]
    ratio = new / norm
    step = new / (bend + ratio * (2.0 * cross + ratio * curve))
    weights[...] = jnp.where(
        lane == 0, alpha + step * (1.0 + ratio), jnp.where(lane == 1, step * alpha, 0.0)
    )
    for copy in pending:
        copy.wait_send()


def finish_kernel(start, r0, w0, z0, weights, answer, residual, held, sems):
    bands = start.shape[0]
    size = bands // FINISH
    copies = []
    for c in range(FINISH):
        rows = pl.ds(c * size, size)
        first, second = weights[rows, 0:1], weights[rows, 1:2]
        held[0, rows] = start[rows] + first * r0[rows] - second * w0[rows]
        held[1, rows] = r0[rows] - first * w0[rows] + second * z0[rows]
        for i, out in enumerate((answer, residual)):
            copy = pltpu.make_async_copy(held.at[i, rows], out.at[0, rows], sems.at[i, c])
            copy.start()
            copies.append(copy)
    for copy in copies:
        copy.wait()


def fused(
    occupied,
    start_guess,
    potential,
    perturbation,
    energy,
    beta_radial,
    beta_slope,
    offset,
    owner,
    site,
    displaced,
):
    slabs = lax.axis_size("dom")
    atoms = owner.shape[0]
    bands, cells = occupied.shape
    every = 4 * bands
    rows = every + 128
    f32, bf16, i32 = jnp.float32, jnp.bfloat16, jnp.int32
    vmem = pl.BlockSpec(memory_space=pltpu.VMEM)
    hbm = pl.BlockSpec(memory_space=pltpu.HBM)
    out = jax.ShapeDtypeStruct((bands, cells), f32)
    dma = pltpu.SemaphoreType.DMA
    points = offset.shape[1]
    state = pl.pallas_call(
        functools.partial(fused_kernel, atoms, slabs),
        out_shape=(out, out, out, out, jax.ShapeDtypeStruct((bands, 128), f32)),
        in_specs=[hbm] * 10 + [pl.BlockSpec(memory_space=pltpu.SMEM)],
        out_specs=(vmem,) * 5,
        scratch_shapes=[
            pltpu.VMEM((bands, cells), f32),
            pltpu.VMEM((cells // 128, 128), f32),
            pltpu.VMEM((1, cells), f32),
            pltpu.VMEM((1, bands), f32),
            pltpu.VMEM((1, points), f32),
            pltpu.VMEM((1, points), f32),
            pltpu.VMEM((3, points), i32),
            pltpu.VMEM((1, atoms), i32),
            pltpu.VMEM((3, atoms), i32),
            pltpu.VMEM((bands, 128), f32),
            pltpu.VMEM((128, cells), f32),
            pltpu.VMEM((PLANE, PLANE), bf16),
            pltpu.VMEM((PLANE, PLANE), bf16),
            pltpu.VMEM((3, bands, cells), f32),
            pltpu.VMEM((rows, cells), bf16),
            pltpu.VMEM((rows, cells), bf16),
            pltpu.VMEM((bands, cells), bf16),
            pltpu.VMEM((bands, cells), bf16),
            pltpu.VMEM((3, 2, bands, cells), f32),
            pltpu.VMEM((3, bands, rows), f32),
            pltpu.VMEM((3, slabs, 8, rows), f32),
            pltpu.VMEM((3, 8, rows), f32),
            pltpu.VMEM((3, bands, rows), f32),
            pltpu.VMEM((8, every), f32),
            pltpu.VMEM((slabs, 8, every), f32),
            pltpu.VMEM((8, 128), f32),
            pltpu.VMEM((slabs, 8, 128), f32),
            dma((5,)),
            dma((5,)),
            dma((3, CHUNKS)),
            dma((3, CHUNKS)),
            dma((3, CHUNKS)),
            dma((3, CHUNKS)),
            dma((3, slabs)),
            dma((3, slabs)),
            dma((3, slabs)),
            dma((3, slabs)),
            dma((slabs,)),
            dma((slabs,)),
            dma((slabs,)),
            dma((slabs,)),
            dma((10,)),
        ],
        compiler_params=pltpu.CompilerParams(
            collective_id=0, has_side_effects=True, vmem_limit_bytes=40 * 1024 * 1024
        ),
    )(
        *(
            pltpu.with_memory_space_constraint(x, pltpu.HBM)
            for x in (
                occupied,
                start_guess[0],
                potential.reshape(cells // 128, 128),
                perturbation,
                energy[None, :],
                beta_radial[None, :],
                beta_slope[None, :],
                offset,
                owner[None, :],
                site,
            )
        ),
        displaced,
    )
    final = jax.ShapeDtypeStruct((1, bands, cells), f32)
    return pl.pallas_call(
        finish_kernel,
        out_shape=(final, final),
        in_specs=[vmem] * 5,
        out_specs=(hbm, hbm),
        scratch_shapes=[pltpu.VMEM((2, bands, cells), f32), dma((2, FINISH))],
        compiler_params=pltpu.CompilerParams(vmem_limit_bytes=16 * 1024 * 1024),
    )(*state)


def local(
    occupied,
    start_guess,
    potential,
    perturbation,
    band_energy,
    beta_radial,
    beta_slope,
    atom_owner,
    atom_site,
    sphere_offset,
    displaced,
):
    slabs = lax.axis_size("dom")
    bands, cells = start_guess.shape[1:]
    atoms = atom_owner.shape[0]
    fits = bands == 8 * slabs and lax.axis_size("band") == 4 and atoms % 16 == 0 and atoms <= 112
    if fits and cells == HALO * PLANE:
        return fused(
            occupied,
            start_guess,
            potential,
            perturbation,
            band_energy,
            beta_radial,
            beta_slope,
            sphere_offset,
            atom_owner,
            atom_site,
            displaced,
        )
    fields = atom_fields(
        slabs, cells, beta_radial, beta_slope, sphere_offset, atom_owner, atom_site, displaced
    )
    answer, residual = plain(
        occupied,
        start_guess[0],
        potential[None, :],
        perturbation,
        band_energy[:, None],
        fields[:atoms],
        fields[atoms : atoms + 8],
        jnp.asarray(plane_matrix()),
    )
    return answer[None], residual[None]


def solution(mesh):
    return jax.shard_map(
        local,
        mesh=mesh,
        in_specs=(
            P("band", "dom"),
            P(None, "band", "dom"),
            P("dom"),
            P(None, "dom"),
            P("band"),
            P(),
            P(),
            P(),
            P(),
            P(),
            P(),
        ),
        out_specs=(P(None, "band", "dom"), P(None, "band", "dom")),
        check_vma=False,
    )
```

```python
import functools
import numpy as np
import jax
import jax.numpy as jnp
from jax import lax
from jax.experimental import pallas as pl
from jax.experimental.pallas import tpu as pltpu
from jax.sharding import PartitionSpec as P

NY = 16
NX = 16
PLANE = NY * NX
HALO = 6
CHUNKS = 8
SUM_AT = 1
FINISH = 4
PIECES = 4
EAGER = 0
DEPTH = 3
RAD = 5

COEF = (
    -5369.0 / 1800.0,
    12.0 / 7.0,
    -15.0 / 56.0,
    10.0 / 189.0,
    -1.0 / 112.0,
    2.0 / 825.0,
    -1.0 / 1386.0,
)
KINETIC = 2.0
SHIFT = 20.0
STRENGTH = 10.0
HIGH = lax.Precision.HIGHEST


def plane_matrix():
    full = np.zeros((PLANE, PLANE), np.float64)
    for y in range(NY):
        for x in range(NX):
            at = y * NX + x
            full[at, at] += 3.0 * COEF[0]
            for d in range(1, 7):
                for s in (d, -d):
                    full[((y + s) % NY) * NX + x, at] += COEF[d]
                    full[y * NX + (x + s) % NX, at] += COEF[d]
    return (-KINETIC * full).astype(np.float32)


def fields_kernel(slabs, depth, radial, slope, offset, owner, site, displaced, out, padded):
    atoms = owner.shape[0]
    planes = slabs * depth
    points = offset.shape[1]
    slab = lax.axis_index("dom")
    rows = lax.broadcasted_iota(jnp.int32, (16, points), 0)
    along_z = rows == offset[0:1, :] + RAD
    in_plane = (offset[1:2, :] & (NY - 1)) * NX + (offset[2:3, :] & (NX - 1))
    hot = jnp.where(
        lax.broadcasted_iota(jnp.int32, (PLANE, points), 0) == in_plane, 1.0, 0.0
    ).astype(jnp.float32)
    left = jnp.concatenate(
        [jnp.where(along_z, radial[...], 0.0), jnp.where(along_z, slope[...], 0.0)], axis=0
    )
    template = lax.dot_general(
        left, hot, (((1,), (1,)), ((), ())), precision=HIGH, preferred_element_type=jnp.float32
    )
    padded[...] = jnp.zeros_like(padded)
    for which in range(2):
        part = template[16 * which : 16 * which + 16]
        padded[which, 0:16, :] = part
        padded[which, planes : planes + 16, :] = part
    column = lax.broadcasted_iota(jnp.int32, (8, PLANE), 1) & (NX - 1)

    def shifted(which, a):
        z = lax.rem(slab * depth + RAD + 2 * planes - owner[a] * depth - site[0, a], planes)
        x = site[2, a]
        turn = site[1, a] * NX + x
        start = pl.multiple_of(lax.div(z, 8) * 8, 8)
        block = pltpu.roll(padded[which, pl.ds(start, 16), :], lax.rem(16 - lax.rem(z, 8), 16), 0)[0:8]
        first = pltpu.roll(block, turn, 1)
        second = pltpu.roll(block, lax.rem(turn + PLANE - NX, PLANE), 1)
        return jnp.where(column >= x, first, second)

    out[atoms:, :] = jnp.zeros((out.shape[0] - atoms, out.shape[1]), jnp.float32)
    for row in range(atoms + 2):
        field = shifted(0, row) if row < atoms else shifted(row - atoms, displaced[0])
        for z in range(depth):
            out[row : row + 1, z * PLANE : (z + 1) * PLANE] = field[z : z + 1]


def place_fields(slab, slabs, depth, atoms, radial, slope, offset, owner, site, displaced, fields):
    planes = slabs * depth
    points = offset.shape[1]
    count = atoms + 8
    rows = lax.broadcasted_iota(jnp.int32, (16, points), 0)
    along_z = rows == offset[0:1, :] + RAD
    in_plane = (offset[1:2, :] & (NY - 1)) * NX + (offset[2:3, :] & (NX - 1))
    hot = jnp.where(
        lax.broadcasted_iota(jnp.int32, (PLANE, points), 0) == in_plane, 1.0, 0.0
    ).astype(jnp.float32)
    left = jnp.concatenate(
        [jnp.where(along_z, radial[...], 0.0), jnp.where(along_z, slope[...], 0.0)], axis=0
    )
    template = lax.dot_general(
        left, hot, (((1,), (1,)), ((), ())), precision=HIGH, preferred_element_type=jnp.float32
    )
    row = lax.broadcasted_iota(jnp.int32, (count, atoms), 0)
    atom = lax.broadcasted_iota(jnp.int32, (count, atoms), 1)
    chosen = atom == jnp.where(row < atoms, row, displaced[0])

    def column(values):
        return jnp.sum(jnp.where(chosen, values, 0), axis=1, keepdims=True)

    centre = column(owner[...]) * depth + column(site[0:1, :])
    turn_y, turn_x = column(site[1:2, :]), column(site[2:3, :])
    row = lax.broadcasted_iota(jnp.int32, (count, 32), 0)
    lane = lax.broadcasted_iota(jnp.int32, (count, 32), 1)
    picks = []
    for z in range(depth):
        at = slab * depth + (z + RAD) - centre
        at = jnp.where(at < 0, at + planes, jnp.where(at >= planes, at - planes, at))
        at = jnp.where(at < 16, at, -32)
        pick = lane == at + jnp.where(row == atoms + 1, 16, 0)
        picks.append(jnp.where(pick & (row < atoms + 2), 1.0, 0.0).astype(jnp.float32))
    value = lax.dot_general(
        jnp.concatenate(picks, axis=0),
        template,
        (((1,), (0,)), ((), ())),
        precision=HIGH,
        preferred_element_type=jnp.float32,
    )
    x = lax.broadcasted_iota(jnp.int32, (count, PLANE), 1) & (NX - 1)
    wide_x = jnp.broadcast_to(turn_x, (count, PLANE))
    wide_y = jnp.broadcast_to(turn_y, (count, PLANE))
    fields[atoms:, :] = jnp.zeros((fields.shape[0] - atoms, fields.shape[1]), jnp.float32)
    for z in range(depth):
        block = value[z * count : (z + 1) * count]
        for d in (1, 2, 4, 8):
            near, far = pltpu.roll(block, d, 1), pltpu.roll(block, PLANE + d - NX, 1)
            block = jnp.where((wide_x & d) != 0, jnp.where(x >= d, near, far), block)
        for d in (1, 2, 4, 8):
            block = jnp.where((wide_y & d) != 0, pltpu.roll(block, d * NX, 1), block)
        fields[0:count, z * PLANE : (z + 1) * PLANE] = block


def atom_fields(slabs, cells, beta_radial, beta_slope, offset, owner, site, displaced):
    atoms = owner.shape[0]
    depth = cells // PLANE
    vmem = pl.BlockSpec(memory_space=pltpu.VMEM)
    smem = pl.BlockSpec(memory_space=pltpu.SMEM)
    return pl.pallas_call(
        functools.partial(fields_kernel, slabs, depth),
        out_shape=jax.ShapeDtypeStruct((max(128, atoms + 16), cells), jnp.float32),
        in_specs=[vmem, vmem, vmem, smem, smem, smem],
        out_specs=vmem,
        scratch_shapes=[pltpu.VMEM((2, slabs * depth + 16, PLANE), jnp.float32)],
        compiler_params=pltpu.CompilerParams(vmem_limit_bytes=16 * 1024 * 1024),
    )(beta_radial[None, :], beta_slope[None, :], offset, owner, site, displaced)


def times(a, b, dims):
    return lax.dot_general(a, b, (dims, ((), ())), precision=HIGH, preferred_element_type=jnp.float32)


def plain(occupied, start, potential, perturbation, energy, beta, pair, in_plane):
    slabs = lax.axis_size("dom")
    bands, cells = start.shape
    depth = cells // PLANE
    total = cells * slabs
    whole = lax.all_gather(occupied, "band", axis=0, tiled=True)
    every = whole.shape[0]
    up = [(i, (i + 1) % slabs) for i in range(slabs)]
    down = [(j, i) for i, j in up]

    def local_part(field):
        before = lax.ppermute(field, "dom", up)
        after = lax.ppermute(field, "dom", down)
        grid = jnp.concatenate([before, field, after], axis=1)
        image = times(field.reshape(bands * depth, PLANE), in_plane, ((1,), (0,))).reshape(bands, cells)
        for d in range(1, 7):
            low = (depth - d) * PLANE
            high = (depth + d) * PLANE
            image += (-KINETIC * COEF[d]) * (grid[:, low : low + cells] + grid[:, high : high + cells])
        return image + (potential - energy) * field

    def correlate(field):
        return jnp.concatenate(
            [times(field, whole, ((1,), (1,))), times(field, beta, ((1,), (1,)))], axis=1
        )

    def operator(field, total_correlation):
        return (
            local_part(field)
            + (SHIFT / total) * times(total_correlation[:, :every], whole, ((1,), (0,)))
            + STRENGTH * times(total_correlation[:, every:], beta, ((1,), (0,)))
        )

    def dot(u, v):
        return jnp.sum(u * v, axis=1, keepdims=True)

    shaped = perturbation * occupied
    first, on_atoms, own, of_all = lax.psum(
        (
            times(shaped - SHIFT * start, whole, ((1,), (1,))),
            times(start, beta, ((1,), (1,))),
            times(occupied, pair, ((1,), (1,))),
            times(pair, whole, ((1,), (1,))),
        ),
        "dom",
    )
    own_radial, own_slope = own[:, 0:1], own[:, 1:2]
    first = first + STRENGTH * (own_radial * of_all[1:2] + own_slope * of_all[0:1])
    residual = (
        times(first * (1.0 / total), whole, ((1,), (0,)))
        - STRENGTH * times(on_atoms, beta, ((1,), (0,)))
        - local_part(start)
        - shaped
        - STRENGTH * (own_radial * pair[1:2] + own_slope * pair[0:1])
    )
    correlation, norm = lax.psum((correlate(residual), dot(residual, residual)), "dom")
    image = operator(residual, correlation)
    correlation, curve = lax.psum((correlate(image), dot(residual, image)), "dom")
    alpha = norm / curve
    again = operator(image, correlation)
    later = residual - alpha * image
    later_image = image - alpha * again
    new, bend, cross = lax.psum((dot(later, later), dot(later, later_image), dot(later, image)), "dom")
    ratio = new / norm
    step = new / (bend + ratio * (2.0 * cross + ratio * curve))
    answer = start + alpha * residual + step * (later + ratio * residual)
    return answer, later - step * (later_image + ratio * image)


NT = (((1,), (1,)), ((), ()))
NN = (((1,), (0,)), ((), ()))
MESH = pl.DeviceIdType.MESH


def parts_of(x):
    high = x.astype(jnp.bfloat16)
    return high, (x - high.astype(jnp.float32)).astype(jnp.bfloat16)


def product(a, b, dims):
    def one(u, v):
        return lax.dot_general(u, v, dims, preferred_element_type=jnp.float32)

    return one(a[0], b[0]) + (one(a[0], b[1]) + one(a[1], b[0]))


def fused_kernel(
    atoms,
    slabs,
    occ_in,
    start_in,
    pot_in,
    pert_in,
    energy_in,
    radial_in,
    slope_in,
    offset_in,
    owner_in,
    site_in,
    displaced,
    start,
    r0,
    w0,
    image,
    weights,
    occ,
    pot,
    pert,
    energy_row,
    radial,
    slope,
    offset,
    owner,
    site,
    energy,
    fields,
    plane_high,
    plane_low,
    whole,
    w_high,
    w_low,
    f_high,
    f_low,
    faces,
    part,
    pieces,
    summed,
    totals,
    last_part,
    last_in,
    band_send,
    band_recv,
    face_send,
    face_recv,
    hand_send,
    hand_recv,
    sum_send,
    sum_recv,
    all_send,
    all_recv,
    last_send,
    last_recv,
    local_sem,
):
    bands, cells = occ.shape
    every = 4 * bands
    total = cells * slabs
    band = lax.axis_index("band")
    slab = lax.axis_index("dom")
    sibling = band + 1 - 2 * (band % 2)
    across = (band + 2) % 4
    barrier = pltpu.get_barrier_semaphore()
    pl.semaphore_signal(barrier, inc=1, device_id={"band": sibling}, device_id_type=MESH)
    pl.semaphore_signal(barrier, inc=1, device_id={"band": across}, device_id_type=MESH)
    peers = [(slab + k) % slabs for k in range(slabs)]
    for k in range(1, slabs):
        pl.semaphore_signal(barrier, inc=1, device_id={"dom": peers[k]}, device_id_type=MESH)
    loads = [
        pltpu.make_async_copy(src, dst, local_sem.at[i])
        for i, (src, dst) in enumerate(
            (
                (offset_in, offset),
                (radial_in, radial),
                (slope_in, slope),
                (owner_in, owner),
                (site_in, site),
                (energy_in, energy_row),
                (pot_in, pot),
                (pert_in, pert),
                (start_in, start),
                (occ_in, occ),
            )
        )
    ]
    for load in loads:
        load.start()
    pl.semaphore_wait(barrier, slabs + 1)

    pending = []

    def send(src, dst, send_sem, recv_sem, device, begin=True):
        copy = pltpu.make_async_remote_copy(
            src_ref=src,
            dst_ref=dst,
            send_sem=send_sem,
            recv_sem=recv_sem,
            device_id=device,
            device_id_type=MESH,
        )
        if begin:
            copy.start()
        pending.append(copy)
        return copy

    chunk = bands // CHUNKS
    side = slab % 2
    beside = slab + 1 - 2 * side
    beyond = (slab + slabs + 2 - 4 * side) % slabs

    def send_face(turn, field, c, begin=True):
        return send(
            field.at[pl.ds(c * chunk, chunk)],
            faces.at[turn, side, pl.ds(c * chunk, chunk)],
            face_send.at[turn, c],
            face_recv.at[turn, c],
            {"dom": beside},
            begin,
        )

    def hand_over(turn, c):
        return send(
            faces.at[turn, 1 - side, pl.ds(c * chunk, chunk)],
            faces.at[turn, side, pl.ds(c * chunk, chunk)],
            hand_send.at[turn, c],
            hand_recv.at[turn, c],
            {"dom": beyond},
        )

    def hand_on(turn, copies, c):
        copies[c].wait_recv()
        copies.append(hand_over(turn, c))

    half = bands // PIECES
    crossing = [
        send(
            occ_in.at[pl.ds(c * half, half)],
            whole.at[1, pl.ds(c * half, half)],
            band_send.at[c],
            band_recv.at[c],
            {"band": across},
        )
        for c in range(PIECES)
    ]
    to_sibling = send(occ_in, whole.at[0], band_send.at[2 * PIECES], band_recv.at[2 * PIECES], {"band": sibling})
    moving = [send_face(0, start_in, c) for c in range(CHUNKS)]

    def hold(row, block):
        high, low = parts_of(block)
        w_high[row : row + block.shape[0], :] = high
        w_low[row : row + block.shape[0], :] = low

    def hold_field(block):
        high, low = parts_of(block)
        f_high[...] = high
        f_low[...] = low

    def plane_image(field, planes):
        for z in planes:
            cut = slice(z * PLANE, (z + 1) * PLANE)
            local_pot = jnp.concatenate(
                [pot[i : i + 1] for i in range(z * PLANE // 128, (z + 1) * PLANE // 128)], axis=1
            )
            image[:, cut] = product(
                (f_high[:, cut], f_low[:, cut]), (plane_high[...], plane_low[...]), NN
            ) + (local_pot - energy[:, 0:1]) * field[:, cut]

    def across_planes(turn, field, c):
        def group(i, carry):
            rows = pl.ds(pl.multiple_of(i * 8, 8), 8)
            grid = [
                ref[rows, z * PLANE : (z + 1) * PLANE]
                for ref in (faces.at[turn, 0], field, faces.at[turn, 1])
                for z in range(HALO)
            ]
            for z in range(HALO):
                cut = slice(z * PLANE, (z + 1) * PLANE)
                value = image[rows, cut]
                for d in range(1, 7):
                    value += (-KINETIC * COEF[d]) * (grid[HALO + z - d] + grid[HALO + z + d])
                image[rows, cut] = value
            return carry

        lax.fori_loop(c * chunk // 8, (c + 1) * chunk // 8, group, 0)

    def start_sum(turn):
        return [
            send(
                part.at[turn, pl.ds(pl.multiple_of(peers[k] * 8, 8), 8)],
                pieces.at[turn, k],
                sum_send.at[turn, k],
                sum_recv.at[turn, k],
                {"dom": peers[k]},
            )
            for k in range(1, slabs)
        ]

    def share_sum(turn, copies):
        mine = pl.ds(pl.multiple_of(slab * 8, 8), 8)
        value = part[turn, mine, :]
        for k in range(1, slabs):
            copies[k - 1].wait_recv()
            value += pieces[turn, k]
        summed[turn] = value
        shared = [
            send(
                summed.at[turn],
                totals.at[turn, mine],
                all_send.at[turn, k],
                all_recv.at[turn, k],
                {"dom": peers[k]},
            )
            for k in range(1, slabs)
        ]
        totals[turn, mine, :] = value
        return shared

    def finish_sum(shared):
        for copy in shared:
            copy.wait_recv()

    lane = lax.broadcasted_iota(jnp.int32, (bands, 128), 1)

    def correlate(rows):
        return product((f_high[...], f_low[...]), (w_high[rows, :], w_low[rows, :]), NT)

    def back(coefficients):
        return product(parts_of(coefficients), (w_high[...], w_low[...]), NN)

    pair = slice(every, every + 128)

    def pair_part(q, block):
        rows = slice(q * bands, (q + 1) * bands)
        mine = product(
            (w_high[rows, :], w_low[rows, :]), (w_high[pair, :], w_low[pair, :]), NT
        )
        if q:
            mine = pltpu.roll(mine, 2 * q, 1)
        at = atoms + 2 * q
        return jnp.where((lane == at) | (lane == at + 1), mine, block)

    one_cell = lax.broadcasted_iota(jnp.int32, (PLANE, PLANE), 0)
    other_cell = lax.broadcasted_iota(jnp.int32, (PLANE, PLANE), 1)
    along_x = (one_cell - other_cell) & (NX - 1)
    along_y = ((one_cell >> 4) - (other_cell >> 4)) & (NY - 1)
    away_x = jnp.minimum(along_x, NX - along_x)
    away_y = jnp.minimum(along_y, NY - along_y)
    away = jnp.where(away_x == 0, away_y, jnp.where(away_y == 0, away_x, NX))
    matrix = jnp.where(away == 0, -KINETIC * 3.0 * COEF[0], 0.0)
    for d in range(1, 7):
        matrix = jnp.where(away == d, -KINETIC * COEF[d], matrix)
    matrix_high, matrix_low = parts_of(matrix.astype(jnp.float32))
    plane_high[...] = matrix_high
    plane_low[...] = matrix_low

    for load in loads[:8]:
        load.wait()
    rows = lax.broadcasted_iota(jnp.int32, (bands, bands), 0)
    columns = lax.broadcasted_iota(jnp.int32, (bands, bands), 1)
    energy[...] = jnp.broadcast_to(
        jnp.sum(jnp.where(rows == columns, energy_row[...], 0.0), axis=1, keepdims=True), (bands, 128)
    )
    place_fields(
        slab, slabs, cells // PLANE, atoms, radial, slope, offset, owner, site, displaced, fields
    )
    for load in loads[8:]:
        load.wait()
    hold(0, occ[...])
    hold(every, fields[...])
    hold_field(start[...])
    plane_image(start, range(HALO))
    hand_on(0, moving, 0)
    hand_on(0, moving, 1)
    ends = slice(every, every + 128)
    on_start = correlate(ends)
    hand_on(0, moving, 2)
    shaped = pert[...] * occ[...]
    hold_field(shaped - SHIFT * start[...])
    to_sibling.wait_recv()
    hold(bands, whole[0])
    hand_on(0, moving, 3)
    part[0, :, 0 : 2 * bands] = correlate(slice(0, 2 * bands))
    on_fields = pair_part(0, pair_part(1, on_start))
    passed = []
    for c in range(PIECES):
        crossing[c].wait_recv()
        passed.append(
            send(
                whole.at[1, pl.ds(c * half, half)],
                whole.at[2, pl.ds(c * half, half)],
                band_send.at[PIECES + c],
                band_recv.at[PIECES + c],
                {"band": sibling},
            )
        )
        hand_on(0, moving, 4 + c)
        hold(2 * bands + c * half, whole[1, c * half : (c + 1) * half])
        if c > 0:
            passed[c - 1].wait_recv()
            hold(3 * bands + (c - 1) * half, whole[2, (c - 1) * half : c * half])
    passed[PIECES - 1].wait_recv()
    hold(4 * bands - half, whole[2, bands - half :])
    part[0, :, 2 * bands : every] = correlate(slice(2 * bands, every))
    part[0, :, every:] = pair_part(2, pair_part(3, on_fields))
    copies = start_sum(0)
    shared = share_sum(0, copies)
    for c in range(CHUNKS):
        moving[CHUNKS + c].wait_recv()
        across_planes(0, start, c)
    finish_sum(shared)
    last = totals[0, :, every:]
    own_radial, own_slope = last[:, atoms : atoms + 1], last[:, atoms + 1 : atoms + 2]
    swapped = jnp.where(
        lane == atoms, own_slope, jnp.where(lane == atoms + 1, own_radial, 0.0)
    )
    of_all = jnp.concatenate(
        [last] + [pltpu.roll(last, 128 - 2 * q, 1) for q in range(1, 4)], axis=0
    )
    first = totals[0, :, 0:every] + STRENGTH * product(parts_of(swapped), parts_of(of_all), NT)
    ends_part = jnp.where(lane < atoms, last, swapped)
    r0[...] = (
        back(jnp.concatenate([first * (1.0 / total), -STRENGTH * ends_part], axis=1))
        - image[...]
        - pert[...] * occ[...]
    )

    def apply(turn, field, scalar, between=None):
        face = [send_face(turn, field, c) for c in range(2)]
        hold_field(field[...])
        part[turn, :, 0:every] = correlate(slice(0, every))
        part[turn, :, every:] = jnp.where(lane == atoms, scalar, correlate(ends))
        copies = start_sum(turn)
        face += [send_face(turn, field, c, False) for c in range(2, CHUNKS)]

        @pl.when(band % 2 == EAGER)
        def _():
            for copy in face[2:]:
                copy.start()

        @pl.when(band % 2 != EAGER)
        def _():
            for copy in face[2:DEPTH]:
                copy.start()

        plane_image(field, range(HALO))
        handed = []
        for c in range(CHUNKS):
            face[c].wait_recv()
            handed.append(hand_over(turn, c))
            if c + DEPTH < CHUNKS:

                @pl.when(band % 2 != EAGER)
                def _():
                    face[c + DEPTH].start()

            if c == SUM_AT:
                shared = share_sum(turn, copies)
            if c >= 4:
                handed[c - 4].wait_recv()
                across_planes(turn, field, c - 4)
        finish_sum(shared)
        if between is not None:
            for c in range(CHUNKS - 4, CHUNKS):
                handed[c].wait_recv()
                across_planes(turn, field, c)
            between(totals[turn, :, every + atoms : every + atoms + 1])
        last = totals[turn, :, every:]
        coefficients = jnp.concatenate(
            [
                totals[turn, :, 0:every] * (SHIFT / total),
                jnp.where(lane < atoms, STRENGTH * last, 0.0),
            ],
            axis=1,
        )
        image[...] += back(coefficients)
        if between is None:
            for c in range(CHUNKS - 4, CHUNKS):
                handed[c].wait_recv()
                across_planes(turn, field, c)
        return last[:, atoms : atoms + 1], coefficients

    def dot(u, v):
        return jnp.sum(u * v, axis=1, keepdims=True)

    norm, _ = apply(1, r0, dot(r0[...], r0[...]))
    w0[...] = image[...]
    eye = jnp.where(
        lax.broadcasted_iota(jnp.int32, (128, 128), 0)
        == lax.broadcasted_iota(jnp.int32, (128, 128), 1),
        1.0,
        0.0,
    ).astype(jnp.float32)
    last_copies = []

    def send_scalars(curve):
        alpha = norm / curve
        later = r0[...] - alpha * w0[...]
        three = jnp.where(
            lane == 0,
            dot(later, later),
            jnp.where(
                lane == 1,
                dot(later, w0[...] - alpha * image[...]),
                jnp.where(lane == 2, dot(later, w0[...]), 0.0),
            ),
        )
        three = jnp.concatenate([three, jnp.zeros((128 - bands, 128), jnp.float32)], axis=0)
        last_part[...] = lax.dot_general(
            eye[0:8], three, NT, precision=HIGH, preferred_element_type=jnp.float32
        )
        last_copies.extend(
            send(last_part, last_in.at[k], last_send.at[k], last_recv.at[k], {"dom": peers[k]})
            for k in range(1, slabs)
        )

    curve, coefficients = apply(2, w0, dot(r0[...], w0[...]), send_scalars)
    alpha = norm / curve
    on_occupied = dot(totals[1] - alpha * totals[2], coefficients)
    value = last_part[...]
    for k in range(1, slabs):
        last_copies[k - 1].wait_recv()
        value += last_in[k]
    three = lax.dot_general(
        eye[0:bands], value, NT, precision=HIGH, preferred_element_type=jnp.float32
    )
    new, cross = three[:, 0:1], three[:, 2:3]
    bend = three[:, 1:2] - alpha * on_occupied
    ratio = new / norm
    step = new / (bend + ratio * (2.0 * cross + ratio * curve))
    weights[...] = jnp.where(
        lane == 0, alpha + step * (1.0 + ratio), jnp.where(lane == 1, step * alpha, 0.0)
    )
    for copy in pending:
        copy.wait_send()


def finish_kernel(start, r0, w0, z0, weights, answer, residual, held, sems):
    bands = start.shape[0]
    size = bands // FINISH
    copies = []
    for c in range(FINISH):
        rows = pl.ds(c * size, size)
        first, second = weights[rows, 0:1], weights[rows, 1:2]
        held[0, rows] = start[rows] + first * r0[rows] - second * w0[rows]
        held[1, rows] = r0[rows] - first * w0[rows] + second * z0[rows]
        for i, out in enumerate((answer, residual)):
            copy = pltpu.make_async_copy(held.at[i, rows], out.at[0, rows], sems.at[i, c])
            copy.start()
            copies.append(copy)
    for copy in copies:
        copy.wait()


def fused(
    occupied,
    start_guess,
    potential,
    perturbation,
    energy,
    beta_radial,
    beta_slope,
    offset,
    owner,
    site,
    displaced,
):
    slabs = lax.axis_size("dom")
    atoms = owner.shape[0]
    bands, cells = occupied.shape
    every = 4 * bands
    rows = every + 128
    f32, bf16, i32 = jnp.float32, jnp.bfloat16, jnp.int32
    vmem = pl.BlockSpec(memory_space=pltpu.VMEM)
    hbm = pl.BlockSpec(memory_space=pltpu.HBM)
    out = jax.ShapeDtypeStruct((bands, cells), f32)
    dma = pltpu.SemaphoreType.DMA
    points = offset.shape[1]
    state = pl.pallas_call(
        functools.partial(fused_kernel, atoms, slabs),
        out_shape=(out, out, out, out, jax.ShapeDtypeStruct((bands, 128), f32)),
        in_specs=[hbm] * 10 + [pl.BlockSpec(memory_space=pltpu.SMEM)],
        out_specs=(vmem,) * 5,
        scratch_shapes=[
            pltpu.VMEM((bands, cells), f32),
            pltpu.VMEM((cells // 128, 128), f32),
            pltpu.VMEM((1, cells), f32),
            pltpu.VMEM((1, bands), f32),
            pltpu.VMEM((1, points), f32),
            pltpu.VMEM((1, points), f32),
            pltpu.VMEM((3, points), i32),
            pltpu.VMEM((1, atoms), i32),
            pltpu.VMEM((3, atoms), i32),
            pltpu.VMEM((bands, 128), f32),
            pltpu.VMEM((128, cells), f32),
            pltpu.VMEM((PLANE, PLANE), bf16),
            pltpu.VMEM((PLANE, PLANE), bf16),
            pltpu.VMEM((3, bands, cells), f32),
            pltpu.VMEM((rows, cells), bf16),
            pltpu.VMEM((rows, cells), bf16),
            pltpu.VMEM((bands, cells), bf16),
            pltpu.VMEM((bands, cells), bf16),
            pltpu.VMEM((3, 2, bands, cells), f32),
            pltpu.VMEM((3, bands, rows), f32),
            pltpu.VMEM((3, slabs, 8, rows), f32),
            pltpu.VMEM((3, 8, rows), f32),
            pltpu.VMEM((3, bands, rows), f32),
            pltpu.VMEM((8, 128), f32),
            pltpu.VMEM((slabs, 8, 128), f32),
            dma((2 * PIECES + 1,)),
            dma((2 * PIECES + 1,)),
            dma((3, CHUNKS)),
            dma((3, CHUNKS)),
            dma((3, CHUNKS)),
            dma((3, CHUNKS)),
            dma((3, slabs)),
            dma((3, slabs)),
            dma((3, slabs)),
            dma((3, slabs)),
            dma((slabs,)),
            dma((slabs,)),
            dma((10,)),
        ],
        compiler_params=pltpu.CompilerParams(
            collective_id=0, has_side_effects=True, vmem_limit_bytes=40 * 1024 * 1024
        ),
    )(
        *(
            pltpu.with_memory_space_constraint(x, pltpu.HBM)
            for x in (
                occupied,
                start_guess[0],
                potential.reshape(cells // 128, 128),
                perturbation,
                energy[None, :],
                beta_radial[None, :],
                beta_slope[None, :],
                offset,
                owner[None, :],
                site,
            )
        ),
        displaced,
    )
    final = jax.ShapeDtypeStruct((1, bands, cells), f32)
    return pl.pallas_call(
        finish_kernel,
        out_shape=(final, final),
        in_specs=[vmem] * 5,
        out_specs=(hbm, hbm),
        scratch_shapes=[pltpu.VMEM((2, bands, cells), f32), dma((2, FINISH))],
        compiler_params=pltpu.CompilerParams(vmem_limit_bytes=16 * 1024 * 1024),
    )(*state)


def local(
    occupied,
    start_guess,
    potential,
    perturbation,
    band_energy,
    beta_radial,
    beta_slope,
    atom_owner,
    atom_site,
    sphere_offset,
    displaced,
):
    slabs = lax.axis_size("dom")
    bands, cells = start_guess.shape[1:]
    atoms = atom_owner.shape[0]
    fits = bands == 8 * slabs and lax.axis_size("band") == 4 and atoms % 16 == 0 and atoms <= 112
    if fits and cells == HALO * PLANE:
        return fused(
            occupied,
            start_guess,
            potential,
            perturbation,
            band_energy,
            beta_radial,
            beta_slope,
            sphere_offset,
            atom_owner,
            atom_site,
            displaced,
        )
    fields = atom_fields(
        slabs, cells, beta_radial, beta_slope, sphere_offset, atom_owner, atom_site, displaced
    )
    answer, residual = plain(
        occupied,
        start_guess[0],
        potential[None, :],
        perturbation,
        band_energy[:, None],
        fields[:atoms],
        fields[atoms : atoms + 8],
        jnp.asarray(plane_matrix()),
    )
    return answer[None], residual[None]


def solution(mesh):
    return jax.shard_map(
        local,
        mesh=mesh,
        in_specs=(
            P("band", "dom"),
            P(None, "band", "dom"),
            P("dom"),
            P(None, "dom"),
            P("band"),
            P(),
            P(),
            P(),
            P(),
            P(),
            P(),
        ),
        out_specs=(P(None, "band", "dom"), P(None, "band", "dom")),
        check_vma=False,
    )
```

```python
import functools
import numpy as np
import jax
import jax.numpy as jnp
from jax import lax
from jax.experimental import pallas as pl
from jax.experimental.pallas import tpu as pltpu
from jax.sharding import PartitionSpec as P

NY = 16
NX = 16
PLANE = NY * NX
HALO = 6
CHUNKS = 8
SUM_AT = 2
FINISH = 4
PIECES = 4
EAGER = 0
DEPTH = 3
RAD = 5

COEF = (
    -5369.0 / 1800.0,
    12.0 / 7.0,
    -15.0 / 56.0,
    10.0 / 189.0,
    -1.0 / 112.0,
    2.0 / 825.0,
    -1.0 / 1386.0,
)
KINETIC = 2.0
SHIFT = 20.0
STRENGTH = 10.0
HIGH = lax.Precision.HIGHEST


def plane_matrix():
    full = np.zeros((PLANE, PLANE), np.float64)
    for y in range(NY):
        for x in range(NX):
            at = y * NX + x
            full[at, at] += 3.0 * COEF[0]
            for d in range(1, 7):
                for s in (d, -d):
                    full[((y + s) % NY) * NX + x, at] += COEF[d]
                    full[y * NX + (x + s) % NX, at] += COEF[d]
    return (-KINETIC * full).astype(np.float32)


def fields_kernel(slabs, depth, radial, slope, offset, owner, site, displaced, out, padded):
    atoms = owner.shape[0]
    planes = slabs * depth
    points = offset.shape[1]
    slab = lax.axis_index("dom")
    rows = lax.broadcasted_iota(jnp.int32, (16, points), 0)
    along_z = rows == offset[0:1, :] + RAD
    in_plane = (offset[1:2, :] & (NY - 1)) * NX + (offset[2:3, :] & (NX - 1))
    hot = jnp.where(
        lax.broadcasted_iota(jnp.int32, (PLANE, points), 0) == in_plane, 1.0, 0.0
    ).astype(jnp.float32)
    left = jnp.concatenate(
        [jnp.where(along_z, radial[...], 0.0), jnp.where(along_z, slope[...], 0.0)], axis=0
    )
    template = lax.dot_general(
        left, hot, (((1,), (1,)), ((), ())), precision=HIGH, preferred_element_type=jnp.float32
    )
    padded[...] = jnp.zeros_like(padded)
    for which in range(2):
        part = template[16 * which : 16 * which + 16]
        padded[which, 0:16, :] = part
        padded[which, planes : planes + 16, :] = part
    column = lax.broadcasted_iota(jnp.int32, (8, PLANE), 1) & (NX - 1)

    def shifted(which, a):
        z = lax.rem(slab * depth + RAD + 2 * planes - owner[a] * depth - site[0, a], planes)
        x = site[2, a]
        turn = site[1, a] * NX + x
        start = pl.multiple_of(lax.div(z, 8) * 8, 8)
        block = pltpu.roll(padded[which, pl.ds(start, 16), :], lax.rem(16 - lax.rem(z, 8), 16), 0)[0:8]
        first = pltpu.roll(block, turn, 1)
        second = pltpu.roll(block, lax.rem(turn + PLANE - NX, PLANE), 1)
        return jnp.where(column >= x, first, second)

    out[atoms:, :] = jnp.zeros((out.shape[0] - atoms, out.shape[1]), jnp.float32)
    for row in range(atoms + 2):
        field = shifted(0, row) if row < atoms else shifted(row - atoms, displaced[0])
        for z in range(depth):
            out[row : row + 1, z * PLANE : (z + 1) * PLANE] = field[z : z + 1]


def place_fields(slab, slabs, depth, atoms, radial, slope, offset, owner, site, displaced, fields):
    planes = slabs * depth
    points = offset.shape[1]
    count = atoms + 8
    rows = lax.broadcasted_iota(jnp.int32, (16, points), 0)
    along_z = rows == offset[0:1, :] + RAD
    in_plane = (offset[1:2, :] & (NY - 1)) * NX + (offset[2:3, :] & (NX - 1))
    hot = jnp.where(
        lax.broadcasted_iota(jnp.int32, (PLANE, points), 0) == in_plane, 1.0, 0.0
    ).astype(jnp.float32)
    left = jnp.concatenate(
        [jnp.where(along_z, radial[...], 0.0), jnp.where(along_z, slope[...], 0.0)], axis=0
    )
    template = lax.dot_general(
        left, hot, (((1,), (1,)), ((), ())), precision=HIGH, preferred_element_type=jnp.float32
    )
    row = lax.broadcasted_iota(jnp.int32, (count, atoms), 0)
    atom = lax.broadcasted_iota(jnp.int32, (count, atoms), 1)
    chosen = atom == jnp.where(row < atoms, row, displaced[0])

    def column(values):
        return jnp.sum(jnp.where(chosen, values, 0), axis=1, keepdims=True)

    centre = column(owner[...]) * depth + column(site[0:1, :])
    turn_y, turn_x = column(site[1:2, :]), column(site[2:3, :])
    row = lax.broadcasted_iota(jnp.int32, (count, 32), 0)
    lane = lax.broadcasted_iota(jnp.int32, (count, 32), 1)
    picks = []
    for z in range(depth):
        at = slab * depth + (z + RAD) - centre
        at = jnp.where(at < 0, at + planes, jnp.where(at >= planes, at - planes, at))
        at = jnp.where(at < 16, at, -32)
        pick = lane == at + jnp.where(row == atoms + 1, 16, 0)
        picks.append(jnp.where(pick & (row < atoms + 2), 1.0, 0.0).astype(jnp.float32))
    value = lax.dot_general(
        jnp.concatenate(picks, axis=0),
        template,
        (((1,), (0,)), ((), ())),
        precision=HIGH,
        preferred_element_type=jnp.float32,
    )
    x = lax.broadcasted_iota(jnp.int32, (count, PLANE), 1) & (NX - 1)
    wide_x = jnp.broadcast_to(turn_x, (count, PLANE))
    wide_y = jnp.broadcast_to(turn_y, (count, PLANE))
    fields[atoms:, :] = jnp.zeros((fields.shape[0] - atoms, fields.shape[1]), jnp.float32)
    for z in range(depth):
        block = value[z * count : (z + 1) * count]
        for d in (1, 2, 4, 8):
            near, far = pltpu.roll(block, d, 1), pltpu.roll(block, PLANE + d - NX, 1)
            block = jnp.where((wide_x & d) != 0, jnp.where(x >= d, near, far), block)
        for d in (1, 2, 4, 8):
            block = jnp.where((wide_y & d) != 0, pltpu.roll(block, d * NX, 1), block)
        fields[0:count, z * PLANE : (z + 1) * PLANE] = block


def atom_fields(slabs, cells, beta_radial, beta_slope, offset, owner, site, displaced):
    atoms = owner.shape[0]
    depth = cells // PLANE
    vmem = pl.BlockSpec(memory_space=pltpu.VMEM)
    smem = pl.BlockSpec(memory_space=pltpu.SMEM)
    return pl.pallas_call(
        functools.partial(fields_kernel, slabs, depth),
        out_shape=jax.ShapeDtypeStruct((max(128, atoms + 16), cells), jnp.float32),
        in_specs=[vmem, vmem, vmem, smem, smem, smem],
        out_specs=vmem,
        scratch_shapes=[pltpu.VMEM((2, slabs * depth + 16, PLANE), jnp.float32)],
        compiler_params=pltpu.CompilerParams(vmem_limit_bytes=16 * 1024 * 1024),
    )(beta_radial[None, :], beta_slope[None, :], offset, owner, site, displaced)


def times(a, b, dims):
    return lax.dot_general(a, b, (dims, ((), ())), precision=HIGH, preferred_element_type=jnp.float32)


def plain(occupied, start, potential, perturbation, energy, beta, pair, in_plane):
    slabs = lax.axis_size("dom")
    bands, cells = start.shape
    depth = cells // PLANE
    total = cells * slabs
    whole = lax.all_gather(occupied, "band", axis=0, tiled=True)
    every = whole.shape[0]
    up = [(i, (i + 1) % slabs) for i in range(slabs)]
    down = [(j, i) for i, j in up]

    def local_part(field):
        before = lax.ppermute(field, "dom", up)
        after = lax.ppermute(field, "dom", down)
        grid = jnp.concatenate([before, field, after], axis=1)
        image = times(field.reshape(bands * depth, PLANE), in_plane, ((1,), (0,))).reshape(bands, cells)
        for d in range(1, 7):
            low = (depth - d) * PLANE
            high = (depth + d) * PLANE
            image += (-KINETIC * COEF[d]) * (grid[:, low : low + cells] + grid[:, high : high + cells])
        return image + (potential - energy) * field

    def correlate(field):
        return jnp.concatenate(
            [times(field, whole, ((1,), (1,))), times(field, beta, ((1,), (1,)))], axis=1
        )

    def operator(field, total_correlation):
        return (
            local_part(field)
            + (SHIFT / total) * times(total_correlation[:, :every], whole, ((1,), (0,)))
            + STRENGTH * times(total_correlation[:, every:], beta, ((1,), (0,)))
        )

    def dot(u, v):
        return jnp.sum(u * v, axis=1, keepdims=True)

    shaped = perturbation * occupied
    first, on_atoms, own, of_all = lax.psum(
        (
            times(shaped - SHIFT * start, whole, ((1,), (1,))),
            times(start, beta, ((1,), (1,))),
            times(occupied, pair, ((1,), (1,))),
            times(pair, whole, ((1,), (1,))),
        ),
        "dom",
    )
    own_radial, own_slope = own[:, 0:1], own[:, 1:2]
    first = first + STRENGTH * (own_radial * of_all[1:2] + own_slope * of_all[0:1])
    residual = (
        times(first * (1.0 / total), whole, ((1,), (0,)))
        - STRENGTH * times(on_atoms, beta, ((1,), (0,)))
        - local_part(start)
        - shaped
        - STRENGTH * (own_radial * pair[1:2] + own_slope * pair[0:1])
    )
    correlation, norm = lax.psum((correlate(residual), dot(residual, residual)), "dom")
    image = operator(residual, correlation)
    correlation, curve = lax.psum((correlate(image), dot(residual, image)), "dom")
    alpha = norm / curve
    again = operator(image, correlation)
    later = residual - alpha * image
    later_image = image - alpha * again
    new, bend, cross = lax.psum((dot(later, later), dot(later, later_image), dot(later, image)), "dom")
    ratio = new / norm
    step = new / (bend + ratio * (2.0 * cross + ratio * curve))
    answer = start + alpha * residual + step * (later + ratio * residual)
    return answer, later - step * (later_image + ratio * image)


NT = (((1,), (1,)), ((), ()))
NN = (((1,), (0,)), ((), ()))
MESH = pl.DeviceIdType.MESH


def parts_of(x):
    high = x.astype(jnp.bfloat16)
    return high, (x - high.astype(jnp.float32)).astype(jnp.bfloat16)


def product(a, b, dims):
    def one(u, v):
        return lax.dot_general(u, v, dims, preferred_element_type=jnp.float32)

    rows = a[0].shape[0]
    both = one(jnp.concatenate(a, axis=0), b[0])
    return both[:rows] + (one(a[0], b[1]) + both[rows:])


def fused_kernel(
    atoms,
    slabs,
    occ_in,
    start_in,
    pot_in,
    pert_in,
    energy_in,
    radial_in,
    slope_in,
    offset_in,
    owner_in,
    site_in,
    displaced,
    start,
    r0,
    w0,
    image,
    weights,
    occ,
    pot,
    pert,
    energy_row,
    radial,
    slope,
    offset,
    owner,
    site,
    energy,
    fields,
    plane_high,
    plane_low,
    whole,
    w_high,
    w_low,
    f_high,
    f_low,
    faces,
    part,
    pieces,
    summed,
    totals,
    last_part,
    last_in,
    band_send,
    band_recv,
    face_send,
    face_recv,
    hand_send,
    hand_recv,
    sum_send,
    sum_recv,
    all_send,
    all_recv,
    last_send,
    last_recv,
    local_sem,
):
    bands, cells = occ.shape
    every = 4 * bands
    total = cells * slabs
    band = lax.axis_index("band")
    slab = lax.axis_index("dom")
    sibling = band + 1 - 2 * (band % 2)
    across = (band + 2) % 4
    barrier = pltpu.get_barrier_semaphore()
    pl.semaphore_signal(barrier, inc=1, device_id={"band": sibling}, device_id_type=MESH)
    pl.semaphore_signal(barrier, inc=1, device_id={"band": across}, device_id_type=MESH)
    peers = [(slab + k) % slabs for k in range(slabs)]
    for k in range(1, slabs):
        pl.semaphore_signal(barrier, inc=1, device_id={"dom": peers[k]}, device_id_type=MESH)
    loads = [
        pltpu.make_async_copy(src, dst, local_sem.at[i])
        for i, (src, dst) in enumerate(
            (
                (offset_in, offset),
                (radial_in, radial),
                (slope_in, slope),
                (owner_in, owner),
                (site_in, site),
                (energy_in, energy_row),
                (pot_in, pot),
                (pert_in, pert),
                (start_in, start),
                (occ_in, occ),
            )
        )
    ]
    for load in loads:
        load.start()
    pl.semaphore_wait(barrier, slabs + 1)

    pending = []

    def send(src, dst, send_sem, recv_sem, device, begin=True):
        copy = pltpu.make_async_remote_copy(
            src_ref=src,
            dst_ref=dst,
            send_sem=send_sem,
            recv_sem=recv_sem,
            device_id=device,
            device_id_type=MESH,
        )
        if begin:
            copy.start()
        pending.append(copy)
        return copy

    chunk = bands // CHUNKS
    side = slab % 2
    beside = slab + 1 - 2 * side
    beyond = (slab + slabs + 2 - 4 * side) % slabs

    def send_face(turn, field, c, begin=True):
        return send(
            field.at[pl.ds(c * chunk, chunk)],
            faces.at[turn, side, pl.ds(c * chunk, chunk)],
            face_send.at[turn, c],
            face_recv.at[turn, c],
            {"dom": beside},
            begin,
        )

    def hand_over(turn, c):
        return send(
            faces.at[turn, 1 - side, pl.ds(c * chunk, chunk)],
            faces.at[turn, side, pl.ds(c * chunk, chunk)],
            hand_send.at[turn, c],
            hand_recv.at[turn, c],
            {"dom": beyond},
        )

    def hand_on(turn, copies, c):
        copies[c].wait_recv()
        copies.append(hand_over(turn, c))

    half = bands // PIECES
    crossing = [
        send(
            occ_in.at[pl.ds(c * half, half)],
            whole.at[1, pl.ds(c * half, half)],
            band_send.at[c],
            band_recv.at[c],
            {"band": across},
        )
        for c in range(PIECES)
    ]
    to_sibling = send(occ_in, whole.at[0], band_send.at[2 * PIECES], band_recv.at[2 * PIECES], {"band": sibling})
    moving = [send_face(0, start_in, c) for c in range(CHUNKS)]

    def hold(row, block):
        high, low = parts_of(block)
        w_high[row : row + block.shape[0], :] = high
        w_low[row : row + block.shape[0], :] = low

    def hold_field(block):
        high, low = parts_of(block)
        f_high[...] = high
        f_low[...] = low

    def plane_image(field, image, planes):
        for z in planes:
            cut = slice(z * PLANE, (z + 1) * PLANE)
            local_pot = jnp.concatenate(
                [pot[i : i + 1] for i in range(z * PLANE // 128, (z + 1) * PLANE // 128)], axis=1
            )
            image[:, cut] = product(
                (f_high[:, cut], f_low[:, cut]), (plane_high[...], plane_low[...]), NN
            ) + (local_pot - energy[:, 0:1]) * field[:, cut]

    def across_planes(turn, field, image, c):
        def group(i, carry):
            rows = pl.ds(pl.multiple_of(i * 8, 8), 8)
            grid = [
                ref[rows, z * PLANE : (z + 1) * PLANE]
                for ref in (faces.at[turn, 0], field, faces.at[turn, 1])
                for z in range(HALO)
            ]
            for z in range(HALO):
                cut = slice(z * PLANE, (z + 1) * PLANE)
                value = image[rows, cut]
                for d in range(1, 7):
                    value += (-KINETIC * COEF[d]) * (grid[HALO + z - d] + grid[HALO + z + d])
                image[rows, cut] = value
            return carry

        lax.fori_loop(c * chunk // 8, (c + 1) * chunk // 8, group, 0)

    def start_sum(turn):
        return [
            send(
                part.at[turn, pl.ds(pl.multiple_of(peers[k] * 8, 8), 8)],
                pieces.at[turn, k],
                sum_send.at[turn, k],
                sum_recv.at[turn, k],
                {"dom": peers[k]},
            )
            for k in range(1, slabs)
        ]

    def share_sum(turn, copies):
        mine = pl.ds(pl.multiple_of(slab * 8, 8), 8)
        value = part[turn, mine, :]
        for k in range(1, slabs):
            copies[k - 1].wait_recv()
            value += pieces[turn, k]
        summed[turn] = value
        shared = [
            send(
                summed.at[turn],
                totals.at[turn, mine],
                all_send.at[turn, k],
                all_recv.at[turn, k],
                {"dom": peers[k]},
            )
            for k in range(1, slabs)
        ]
        totals[turn, mine, :] = value
        return shared

    def finish_sum(shared):
        for copy in shared:
            copy.wait_recv()

    lane = lax.broadcasted_iota(jnp.int32, (bands, 128), 1)

    def correlate(rows):
        return product((f_high[...], f_low[...]), (w_high[rows, :], w_low[rows, :]), NT)

    def back(coefficients):
        return product(parts_of(coefficients), (w_high[...], w_low[...]), NN)

    pair = slice(every, every + 128)

    def pair_part(q, block):
        rows = slice(q * bands, (q + 2) * bands)
        both = product(
            (w_high[rows, :], w_low[rows, :]), (w_high[pair, :], w_low[pair, :]), NT
        )
        for i in range(2):
            mine = both[i * bands : (i + 1) * bands]
            if q + i:
                mine = pltpu.roll(mine, 2 * (q + i), 1)
            at = atoms + 2 * (q + i)
            block = jnp.where((lane == at) | (lane == at + 1), mine, block)
        return block

    one_cell = lax.broadcasted_iota(jnp.int32, (PLANE, PLANE), 0)
    other_cell = lax.broadcasted_iota(jnp.int32, (PLANE, PLANE), 1)
    along_x = (one_cell - other_cell) & (NX - 1)
    along_y = ((one_cell >> 4) - (other_cell >> 4)) & (NY - 1)
    away_x = jnp.minimum(along_x, NX - along_x)
    away_y = jnp.minimum(along_y, NY - along_y)
    away = jnp.where(away_x == 0, away_y, jnp.where(away_y == 0, away_x, NX))
    matrix = jnp.where(away == 0, -KINETIC * 3.0 * COEF[0], 0.0)
    for d in range(1, 7):
        matrix = jnp.where(away == d, -KINETIC * COEF[d], matrix)
    matrix_high, matrix_low = parts_of(matrix.astype(jnp.float32))
    plane_high[...] = matrix_high
    plane_low[...] = matrix_low

    for load in loads[:8]:
        load.wait()
    rows = lax.broadcasted_iota(jnp.int32, (bands, bands), 0)
    columns = lax.broadcasted_iota(jnp.int32, (bands, bands), 1)
    energy[...] = jnp.broadcast_to(
        jnp.sum(jnp.where(rows == columns, energy_row[...], 0.0), axis=1, keepdims=True), (bands, 128)
    )
    place_fields(
        slab, slabs, cells // PLANE, atoms, radial, slope, offset, owner, site, displaced, fields
    )
    for load in loads[8:]:
        load.wait()
    hold(0, occ[...])
    hold(every, fields[...])
    hold_field(start[...])
    plane_image(start, image, range(HALO))
    hand_on(0, moving, 0)
    hand_on(0, moving, 1)
    ends = slice(every, every + 128)
    on_start = correlate(ends)
    hand_on(0, moving, 2)
    shaped = pert[...] * occ[...]
    hold_field(shaped - SHIFT * start[...])
    to_sibling.wait_recv()
    hold(bands, whole[0])
    hand_on(0, moving, 3)
    part[0, :, 0 : 2 * bands] = correlate(slice(0, 2 * bands))
    on_fields = pair_part(0, on_start)
    passed = []
    for c in range(PIECES):
        crossing[c].wait_recv()
        passed.append(
            send(
                whole.at[1, pl.ds(c * half, half)],
                whole.at[2, pl.ds(c * half, half)],
                band_send.at[PIECES + c],
                band_recv.at[PIECES + c],
                {"band": sibling},
            )
        )
        hand_on(0, moving, 4 + c)
        hold(2 * bands + c * half, whole[1, c * half : (c + 1) * half])
        if c > 0:
            passed[c - 1].wait_recv()
            hold(3 * bands + (c - 1) * half, whole[2, (c - 1) * half : c * half])
    passed[PIECES - 1].wait_recv()
    hold(4 * bands - half, whole[2, bands - half :])
    part[0, :, 2 * bands : every] = correlate(slice(2 * bands, every))
    part[0, :, every:] = pair_part(2, on_fields)
    copies = start_sum(0)
    shared = share_sum(0, copies)
    for c in range(CHUNKS):
        moving[CHUNKS + c].wait_recv()
        across_planes(0, start, image, c)
    finish_sum(shared)
    last = totals[0, :, every:]
    own_radial, own_slope = last[:, atoms : atoms + 1], last[:, atoms + 1 : atoms + 2]
    swapped = jnp.where(
        lane == atoms, own_slope, jnp.where(lane == atoms + 1, own_radial, 0.0)
    )
    of_all = jnp.concatenate(
        [last] + [pltpu.roll(last, 128 - 2 * q, 1) for q in range(1, 4)], axis=0
    )
    first = totals[0, :, 0:every] + STRENGTH * product(parts_of(swapped), parts_of(of_all), NT)
    ends_part = jnp.where(lane < atoms, last, swapped)
    projected = back(jnp.concatenate([first * (1.0 / total), -STRENGTH * ends_part], axis=1))
    early = []
    for rows in (slice(0, 2 * chunk), slice(2 * chunk, bands)):
        r0[rows] = projected[rows] - image[rows] - pert[...] * occ[rows]
        if not early:
            early = [send_face(1, r0, c) for c in range(2)]

    def apply(turn, field, image, early, scalar, between=None):
        face = list(early)
        hold_field(field[...])
        part[turn, :, 0:every] = correlate(slice(0, every))
        part[turn, :, every:] = jnp.where(lane == atoms, scalar, correlate(ends))
        copies = start_sum(turn)
        face += [send_face(turn, field, c, False) for c in range(2, CHUNKS)]

        @pl.when(band % 2 == EAGER)
        def _():
            for copy in face[2:]:
                copy.start()

        @pl.when(band % 2 != EAGER)
        def _():
            for copy in face[2:DEPTH]:
                copy.start()

        plane_image(field, image, range(HALO))
        handed = []
        for c in range(CHUNKS):
            face[c].wait_recv()
            handed.append(hand_over(turn, c))
            if c + DEPTH < CHUNKS:

                @pl.when(band % 2 != EAGER)
                def _():
                    face[c + DEPTH].start()

            if c == SUM_AT:
                shared = share_sum(turn, copies)
            if c >= 4:
                handed[c - 4].wait_recv()
                across_planes(turn, field, image, c - 4)
        finish_sum(shared)
        if between is not None:
            for c in range(CHUNKS - 4, CHUNKS):
                handed[c].wait_recv()
                across_planes(turn, field, image, c)
            between(totals[turn, :, every + atoms : every + atoms + 1])
        last = totals[turn, :, every:]
        coefficients = jnp.concatenate(
            [
                totals[turn, :, 0:every] * (SHIFT / total),
                jnp.where(lane < atoms, STRENGTH * last, 0.0),
            ],
            axis=1,
        )
        image[...] += back(coefficients)
        if between is None:
            ahead.extend(send_face(turn + 1, image, c) for c in range(2))
            for c in range(CHUNKS - 4, CHUNKS):
                handed[c].wait_recv()
                across_planes(turn, field, image, c)
        return last[:, atoms : atoms + 1], coefficients

    def dot(u, v):
        return jnp.sum(u * v, axis=1, keepdims=True)

    ahead = []
    norm, _ = apply(1, r0, w0, early, dot(r0[...], r0[...]))
    eye = jnp.where(
        lax.broadcasted_iota(jnp.int32, (128, 128), 0)
        == lax.broadcasted_iota(jnp.int32, (128, 128), 1),
        1.0,
        0.0,
    ).astype(jnp.float32)
    last_copies = []

    def send_scalars(curve):
        alpha = norm / curve
        later = r0[...] - alpha * w0[...]
        three = jnp.where(
            lane == 0,
            dot(later, later),
            jnp.where(
                lane == 1,
                dot(later, w0[...] - alpha * image[...]),
                jnp.where(lane == 2, dot(later, w0[...]), 0.0),
            ),
        )
        three = jnp.concatenate([three, jnp.zeros((128 - bands, 128), jnp.float32)], axis=0)
        last_part[...] = lax.dot_general(
            eye[0:8], three, NT, precision=HIGH, preferred_element_type=jnp.float32
        )
        last_copies.extend(
            send(last_part, last_in.at[k], last_send.at[k], last_recv.at[k], {"dom": peers[k]})
            for k in range(1, slabs)
        )

    curve, coefficients = apply(2, w0, image, ahead, dot(r0[...], w0[...]), send_scalars)
    alpha = norm / curve
    on_occupied = dot(totals[1] - alpha * totals[2], coefficients)
    value = last_part[...]
    for k in range(1, slabs):
        last_copies[k - 1].wait_recv()
        value += last_in[k]
    three = lax.dot_general(
        eye[0:bands], value, NT, precision=HIGH, preferred_element_type=jnp.float32
    )
    new, cross = three[:, 0:1], three[:, 2:3]
    bend = three[:, 1:2] - alpha * on_occupied
    ratio = new / norm
    step = new / (bend + ratio * (2.0 * cross + ratio * curve))
    weights[...] = jnp.where(
        lane == 0, alpha + step * (1.0 + ratio), jnp.where(lane == 1, step * alpha, 0.0)
    )
    for copy in pending:
        copy.wait_send()


def finish_kernel(start, r0, w0, z0, weights, answer, residual, held, sems):
    bands = start.shape[0]
    size = bands // FINISH
    copies = []
    for c in range(FINISH):
        rows = pl.ds(c * size, size)
        first, second = weights[rows, 0:1], weights[rows, 1:2]
        held[0, rows] = start[rows] + first * r0[rows] - second * w0[rows]
        held[1, rows] = r0[rows] - first * w0[rows] + second * z0[rows]
        for i, out in enumerate((answer, residual)):
            copy = pltpu.make_async_copy(held.at[i, rows], out.at[0, rows], sems.at[i, c])
            copy.start()
            copies.append(copy)
    for copy in copies:
        copy.wait()


def fused(
    occupied,
    start_guess,
    potential,
    perturbation,
    energy,
    beta_radial,
    beta_slope,
    offset,
    owner,
    site,
    displaced,
):
    slabs = lax.axis_size("dom")
    atoms = owner.shape[0]
    bands, cells = occupied.shape
    every = 4 * bands
    rows = every + 128
    f32, bf16, i32 = jnp.float32, jnp.bfloat16, jnp.int32
    vmem = pl.BlockSpec(memory_space=pltpu.VMEM)
    hbm = pl.BlockSpec(memory_space=pltpu.HBM)
    out = jax.ShapeDtypeStruct((bands, cells), f32)
    dma = pltpu.SemaphoreType.DMA
    points = offset.shape[1]
    state = pl.pallas_call(
        functools.partial(fused_kernel, atoms, slabs),
        out_shape=(out, out, out, out, jax.ShapeDtypeStruct((bands, 128), f32)),
        in_specs=[hbm] * 10 + [pl.BlockSpec(memory_space=pltpu.SMEM)],
        out_specs=(vmem,) * 5,
        scratch_shapes=[
            pltpu.VMEM((bands, cells), f32),
            pltpu.VMEM((cells // 128, 128), f32),
            pltpu.VMEM((1, cells), f32),
            pltpu.VMEM((1, bands), f32),
            pltpu.VMEM((1, points), f32),
            pltpu.VMEM((1, points), f32),
            pltpu.VMEM((3, points), i32),
            pltpu.VMEM((1, atoms), i32),
            pltpu.VMEM((3, atoms), i32),
            pltpu.VMEM((bands, 128), f32),
            pltpu.VMEM((128, cells), f32),
            pltpu.VMEM((PLANE, PLANE), bf16),
            pltpu.VMEM((PLANE, PLANE), bf16),
            pltpu.VMEM((3, bands, cells), f32),
            pltpu.VMEM((rows, cells), bf16),
            pltpu.VMEM((rows, cells), bf16),
            pltpu.VMEM((bands, cells), bf16),
            pltpu.VMEM((bands, cells), bf16),
            pltpu.VMEM((3, 2, bands, cells), f32),
            pltpu.VMEM((3, bands, rows), f32),
            pltpu.VMEM((3, slabs, 8, rows), f32),
            pltpu.VMEM((3, 8, rows), f32),
            pltpu.VMEM((3, bands, rows), f32),
            pltpu.VMEM((8, 128), f32),
            pltpu.VMEM((slabs, 8, 128), f32),
            dma((2 * PIECES + 1,)),
            dma((2 * PIECES + 1,)),
            dma((3, CHUNKS)),
            dma((3, CHUNKS)),
            dma((3, CHUNKS)),
            dma((3, CHUNKS)),
            dma((3, slabs)),
            dma((3, slabs)),
            dma((3, slabs)),
            dma((3, slabs)),
            dma((slabs,)),
            dma((slabs,)),
            dma((10,)),
        ],
        compiler_params=pltpu.CompilerParams(
            collective_id=0, has_side_effects=True, vmem_limit_bytes=40 * 1024 * 1024
        ),
    )(
        *(
            pltpu.with_memory_space_constraint(x, pltpu.HBM)
            for x in (
                occupied,
                start_guess[0],
                potential.reshape(cells // 128, 128),
                perturbation,
                energy[None, :],
                beta_radial[None, :],
                beta_slope[None, :],
                offset,
                owner[None, :],
                site,
            )
        ),
        displaced,
    )
    final = jax.ShapeDtypeStruct((1, bands, cells), f32)
    return pl.pallas_call(
        finish_kernel,
        out_shape=(final, final),
        in_specs=[vmem] * 5,
        out_specs=(hbm, hbm),
        scratch_shapes=[pltpu.VMEM((2, bands, cells), f32), dma((2, FINISH))],
        compiler_params=pltpu.CompilerParams(vmem_limit_bytes=16 * 1024 * 1024),
    )(*state)


def local(
    occupied,
    start_guess,
    potential,
    perturbation,
    band_energy,
    beta_radial,
    beta_slope,
    atom_owner,
    atom_site,
    sphere_offset,
    displaced,
):
    slabs = lax.axis_size("dom")
    bands, cells = start_guess.shape[1:]
    atoms = atom_owner.shape[0]
    fits = bands == 8 * slabs and lax.axis_size("band") == 4 and atoms % 16 == 0 and atoms <= 112
    if fits and cells == HALO * PLANE:
        return fused(
            occupied,
            start_guess,
            potential,
            perturbation,
            band_energy,
            beta_radial,
            beta_slope,
            sphere_offset,
            atom_owner,
            atom_site,
            displaced,
        )
    fields = atom_fields(
        slabs, cells, beta_radial, beta_slope, sphere_offset, atom_owner, atom_site, displaced
    )
    answer, residual = plain(
        occupied,
        start_guess[0],
        potential[None, :],
        perturbation,
        band_energy[:, None],
        fields[:atoms],
        fields[atoms : atoms + 8],
        jnp.asarray(plane_matrix()),
    )
    return answer[None], residual[None]


def solution(mesh):
    return jax.shard_map(
        local,
        mesh=mesh,
        in_specs=(
            P("band", "dom"),
            P(None, "band", "dom"),
            P("dom"),
            P(None, "dom"),
            P("band"),
            P(),
            P(),
            P(),
            P(),
            P(),
            P(),
        ),
        out_specs=(P(None, "band", "dom"), P(None, "band", "dom")),
        check_vma=False,
    )
```

```python
import functools
import numpy as np
import jax
import jax.numpy as jnp
from jax import lax
from jax.experimental import pallas as pl
from jax.experimental.pallas import tpu as pltpu
from jax.sharding import PartitionSpec as P

NY = 16
NX = 16
PLANE = NY * NX
HALO = 6
CHUNKS = 8
SUM_AT = 2
FINISH = 4
PIECES = 4
EAGER = 0
DEPTH = 5
RAD = 5

COEF = (
    -5369.0 / 1800.0,
    12.0 / 7.0,
    -15.0 / 56.0,
    10.0 / 189.0,
    -1.0 / 112.0,
    2.0 / 825.0,
    -1.0 / 1386.0,
)
KINETIC = 2.0
SHIFT = 20.0
STRENGTH = 10.0
HIGH = lax.Precision.HIGHEST


def plane_matrix():
    full = np.zeros((PLANE, PLANE), np.float64)
    for y in range(NY):
        for x in range(NX):
            at = y * NX + x
            full[at, at] += 3.0 * COEF[0]
            for d in range(1, 7):
                for s in (d, -d):
                    full[((y + s) % NY) * NX + x, at] += COEF[d]
                    full[y * NX + (x + s) % NX, at] += COEF[d]
    return (-KINETIC * full).astype(np.float32)


def fields_kernel(slabs, depth, radial, slope, offset, owner, site, displaced, out, padded):
    atoms = owner.shape[0]
    planes = slabs * depth
    points = offset.shape[1]
    slab = lax.axis_index("dom")
    rows = lax.broadcasted_iota(jnp.int32, (16, points), 0)
    along_z = rows == offset[0:1, :] + RAD
    in_plane = (offset[1:2, :] & (NY - 1)) * NX + (offset[2:3, :] & (NX - 1))
    hot = jnp.where(
        lax.broadcasted_iota(jnp.int32, (PLANE, points), 0) == in_plane, 1.0, 0.0
    ).astype(jnp.float32)
    left = jnp.concatenate(
        [jnp.where(along_z, radial[...], 0.0), jnp.where(along_z, slope[...], 0.0)], axis=0
    )
    template = lax.dot_general(
        left, hot, (((1,), (1,)), ((), ())), precision=HIGH, preferred_element_type=jnp.float32
    )
    padded[...] = jnp.zeros_like(padded)
    for which in range(2):
        part = template[16 * which : 16 * which + 16]
        padded[which, 0:16, :] = part
        padded[which, planes : planes + 16, :] = part
    column = lax.broadcasted_iota(jnp.int32, (8, PLANE), 1) & (NX - 1)

    def shifted(which, a):
        z = lax.rem(slab * depth + RAD + 2 * planes - owner[a] * depth - site[0, a], planes)
        x = site[2, a]
        turn = site[1, a] * NX + x
        start = pl.multiple_of(lax.div(z, 8) * 8, 8)
        block = pltpu.roll(padded[which, pl.ds(start, 16), :], lax.rem(16 - lax.rem(z, 8), 16), 0)[0:8]
        first = pltpu.roll(block, turn, 1)
        second = pltpu.roll(block, lax.rem(turn + PLANE - NX, PLANE), 1)
        return jnp.where(column >= x, first, second)

    out[atoms:, :] = jnp.zeros((out.shape[0] - atoms, out.shape[1]), jnp.float32)
    for row in range(atoms + 2):
        field = shifted(0, row) if row < atoms else shifted(row - atoms, displaced[0])
        for z in range(depth):
            out[row : row + 1, z * PLANE : (z + 1) * PLANE] = field[z : z + 1]


def place_fields(slab, slabs, depth, atoms, radial, slope, offset, owner, site, displaced, fields):
    planes = slabs * depth
    points = offset.shape[1]
    count = atoms + 8
    rows = lax.broadcasted_iota(jnp.int32, (16, points), 0)
    along_z = rows == offset[0:1, :] + RAD
    in_plane = (offset[1:2, :] & (NY - 1)) * NX + (offset[2:3, :] & (NX - 1))
    hot = jnp.where(
        lax.broadcasted_iota(jnp.int32, (PLANE, points), 0) == in_plane, 1.0, 0.0
    ).astype(jnp.float32)
    left = jnp.concatenate(
        [jnp.where(along_z, radial[...], 0.0), jnp.where(along_z, slope[...], 0.0)], axis=0
    )
    template = lax.dot_general(
        left, hot, (((1,), (1,)), ((), ())), precision=HIGH, preferred_element_type=jnp.float32
    )
    row = lax.broadcasted_iota(jnp.int32, (count, atoms), 0)
    atom = lax.broadcasted_iota(jnp.int32, (count, atoms), 1)
    chosen = atom == jnp.where(row < atoms, row, displaced[0])

    def column(values):
        return jnp.sum(jnp.where(chosen, values, 0), axis=1, keepdims=True)

    centre = column(owner[...]) * depth + column(site[0:1, :])
    turn_y, turn_x = column(site[1:2, :]), column(site[2:3, :])
    row = lax.broadcasted_iota(jnp.int32, (count, 32), 0)
    lane = lax.broadcasted_iota(jnp.int32, (count, 32), 1)
    picks = []
    for z in range(depth):
        at = slab * depth + (z + RAD) - centre
        at = jnp.where(at < 0, at + planes, jnp.where(at >= planes, at - planes, at))
        at = jnp.where(at < 16, at, -32)
        pick = lane == at + jnp.where(row == atoms + 1, 16, 0)
        picks.append(jnp.where(pick & (row < atoms + 2), 1.0, 0.0).astype(jnp.float32))
    value = lax.dot_general(
        jnp.concatenate(picks, axis=0),
        template,
        (((1,), (0,)), ((), ())),
        precision=HIGH,
        preferred_element_type=jnp.float32,
    )
    x = lax.broadcasted_iota(jnp.int32, (count, PLANE), 1) & (NX - 1)
    wide_x = jnp.broadcast_to(turn_x, (count, PLANE))
    wide_y = jnp.broadcast_to(turn_y, (count, PLANE))
    fields[atoms:, :] = jnp.zeros((fields.shape[0] - atoms, fields.shape[1]), jnp.float32)
    for z in range(depth):
        block = value[z * count : (z + 1) * count]
        for d in (1, 2, 4, 8):
            near, far = pltpu.roll(block, d, 1), pltpu.roll(block, PLANE + d - NX, 1)
            block = jnp.where((wide_x & d) != 0, jnp.where(x >= d, near, far), block)
        for d in (1, 2, 4, 8):
            block = jnp.where((wide_y & d) != 0, pltpu.roll(block, d * NX, 1), block)
        fields[0:count, z * PLANE : (z + 1) * PLANE] = block


def atom_fields(slabs, cells, beta_radial, beta_slope, offset, owner, site, displaced):
    atoms = owner.shape[0]
    depth = cells // PLANE
    vmem = pl.BlockSpec(memory_space=pltpu.VMEM)
    smem = pl.BlockSpec(memory_space=pltpu.SMEM)
    return pl.pallas_call(
        functools.partial(fields_kernel, slabs, depth),
        out_shape=jax.ShapeDtypeStruct((max(128, atoms + 16), cells), jnp.float32),
        in_specs=[vmem, vmem, vmem, smem, smem, smem],
        out_specs=vmem,
        scratch_shapes=[pltpu.VMEM((2, slabs * depth + 16, PLANE), jnp.float32)],
        compiler_params=pltpu.CompilerParams(vmem_limit_bytes=16 * 1024 * 1024),
    )(beta_radial[None, :], beta_slope[None, :], offset, owner, site, displaced)


def times(a, b, dims):
    return lax.dot_general(a, b, (dims, ((), ())), precision=HIGH, preferred_element_type=jnp.float32)


def plain(occupied, start, potential, perturbation, energy, beta, pair, in_plane):
    slabs = lax.axis_size("dom")
    bands, cells = start.shape
    depth = cells // PLANE
    total = cells * slabs
    whole = lax.all_gather(occupied, "band", axis=0, tiled=True)
    every = whole.shape[0]
    up = [(i, (i + 1) % slabs) for i in range(slabs)]
    down = [(j, i) for i, j in up]

    def local_part(field):
        before = lax.ppermute(field, "dom", up)
        after = lax.ppermute(field, "dom", down)
        grid = jnp.concatenate([before, field, after], axis=1)
        image = times(field.reshape(bands * depth, PLANE), in_plane, ((1,), (0,))).reshape(bands, cells)
        for d in range(1, 7):
            low = (depth - d) * PLANE
            high = (depth + d) * PLANE
            image += (-KINETIC * COEF[d]) * (grid[:, low : low + cells] + grid[:, high : high + cells])
        return image + (potential - energy) * field

    def correlate(field):
        return jnp.concatenate(
            [times(field, whole, ((1,), (1,))), times(field, beta, ((1,), (1,)))], axis=1
        )

    def operator(field, total_correlation):
        return (
            local_part(field)
            + (SHIFT / total) * times(total_correlation[:, :every], whole, ((1,), (0,)))
            + STRENGTH * times(total_correlation[:, every:], beta, ((1,), (0,)))
        )

    def dot(u, v):
        return jnp.sum(u * v, axis=1, keepdims=True)

    shaped = perturbation * occupied
    first, on_atoms, own, of_all = lax.psum(
        (
            times(shaped - SHIFT * start, whole, ((1,), (1,))),
            times(start, beta, ((1,), (1,))),
            times(occupied, pair, ((1,), (1,))),
            times(pair, whole, ((1,), (1,))),
        ),
        "dom",
    )
    own_radial, own_slope = own[:, 0:1], own[:, 1:2]
    first = first + STRENGTH * (own_radial * of_all[1:2] + own_slope * of_all[0:1])
    residual = (
        times(first * (1.0 / total), whole, ((1,), (0,)))
        - STRENGTH * times(on_atoms, beta, ((1,), (0,)))
        - local_part(start)
        - shaped
        - STRENGTH * (own_radial * pair[1:2] + own_slope * pair[0:1])
    )
    correlation, norm = lax.psum((correlate(residual), dot(residual, residual)), "dom")
    image = operator(residual, correlation)
    correlation, curve = lax.psum((correlate(image), dot(residual, image)), "dom")
    alpha = norm / curve
    again = operator(image, correlation)
    later = residual - alpha * image
    later_image = image - alpha * again
    new, bend, cross = lax.psum((dot(later, later), dot(later, later_image), dot(later, image)), "dom")
    ratio = new / norm
    step = new / (bend + ratio * (2.0 * cross + ratio * curve))
    answer = start + alpha * residual + step * (later + ratio * residual)
    return answer, later - step * (later_image + ratio * image)


NT = (((1,), (1,)), ((), ()))
NN = (((1,), (0,)), ((), ()))
MESH = pl.DeviceIdType.MESH


def parts_of(x):
    high = x.astype(jnp.bfloat16)
    return high, (x - high.astype(jnp.float32)).astype(jnp.bfloat16)


def product(a, b, dims):
    def one(u, v):
        return lax.dot_general(u, v, dims, preferred_element_type=jnp.float32)

    rows = a[0].shape[0]
    both = one(jnp.concatenate(a, axis=0), b[0])
    return both[:rows] + (one(a[0], b[1]) + both[rows:])


def fused_kernel(
    atoms,
    slabs,
    occ_in,
    start_in,
    pot_in,
    pert_in,
    energy_in,
    radial_in,
    slope_in,
    offset_in,
    owner_in,
    site_in,
    displaced,
    start,
    r0,
    w0,
    image,
    weights,
    occ,
    pot,
    pert,
    energy_row,
    radial,
    slope,
    offset,
    owner,
    site,
    energy,
    fields,
    plane_high,
    plane_low,
    whole,
    w_high,
    w_low,
    f_high,
    f_low,
    faces,
    part,
    pieces,
    summed,
    totals,
    last_part,
    last_in,
    band_send,
    band_recv,
    face_send,
    face_recv,
    hand_send,
    hand_recv,
    sum_send,
    sum_recv,
    all_send,
    all_recv,
    last_send,
    last_recv,
    local_sem,
):
    bands, cells = occ.shape
    every = 4 * bands
    total = cells * slabs
    band = lax.axis_index("band")
    slab = lax.axis_index("dom")
    sibling = band + 1 - 2 * (band % 2)
    across = (band + 2) % 4
    barrier = pltpu.get_barrier_semaphore()
    pl.semaphore_signal(barrier, inc=1, device_id={"band": sibling}, device_id_type=MESH)
    pl.semaphore_signal(barrier, inc=1, device_id={"band": across}, device_id_type=MESH)
    peers = [(slab + k) % slabs for k in range(slabs)]
    for k in range(1, slabs):
        pl.semaphore_signal(barrier, inc=1, device_id={"dom": peers[k]}, device_id_type=MESH)
    loads = [
        pltpu.make_async_copy(src, dst, local_sem.at[i])
        for i, (src, dst) in enumerate(
            (
                (offset_in, offset),
                (radial_in, radial),
                (slope_in, slope),
                (owner_in, owner),
                (site_in, site),
                (energy_in, energy_row),
                (pot_in, pot),
                (pert_in, pert),
                (start_in, start),
                (occ_in, occ),
            )
        )
    ]
    for load in loads:
        load.start()
    pl.semaphore_wait(barrier, slabs + 1)

    pending = []

    def send(src, dst, send_sem, recv_sem, device, begin=True):
        copy = pltpu.make_async_remote_copy(
            src_ref=src,
            dst_ref=dst,
            send_sem=send_sem,
            recv_sem=recv_sem,
            device_id=device,
            device_id_type=MESH,
        )
        if begin:
            copy.start()
        pending.append(copy)
        return copy

    chunk = bands // CHUNKS
    side = slab % 2
    beside = slab + 1 - 2 * side
    beyond = (slab + slabs + 2 - 4 * side) % slabs

    def send_face(turn, field, c, begin=True):
        return send(
            field.at[pl.ds(c * chunk, chunk)],
            faces.at[turn, side, pl.ds(c * chunk, chunk)],
            face_send.at[turn, c],
            face_recv.at[turn, c],
            {"dom": beside},
            begin,
        )

    def hand_over(turn, c):
        return send(
            faces.at[turn, 1 - side, pl.ds(c * chunk, chunk)],
            faces.at[turn, side, pl.ds(c * chunk, chunk)],
            hand_send.at[turn, c],
            hand_recv.at[turn, c],
            {"dom": beyond},
        )

    def hand_on(turn, copies, c):
        copies[c].wait_recv()
        copies.append(hand_over(turn, c))

    half = bands // PIECES
    crossing = [
        send(
            occ_in.at[pl.ds(c * half, half)],
            whole.at[1, pl.ds(c * half, half)],
            band_send.at[c],
            band_recv.at[c],
            {"band": across},
        )
        for c in range(PIECES)
    ]
    to_sibling = send(occ_in, whole.at[0], band_send.at[2 * PIECES], band_recv.at[2 * PIECES], {"band": sibling})
    moving = [send_face(0, start_in, c) for c in range(CHUNKS)]

    def hold(row, block):
        high, low = parts_of(block)
        w_high[row : row + block.shape[0], :] = high
        w_low[row : row + block.shape[0], :] = low

    def hold_field(block):
        high, low = parts_of(block)
        f_high[...] = high
        f_low[...] = low

    def plane_image(field, image, planes):
        for z in planes:
            cut = slice(z * PLANE, (z + 1) * PLANE)
            local_pot = jnp.concatenate(
                [pot[i : i + 1] for i in range(z * PLANE // 128, (z + 1) * PLANE // 128)], axis=1
            )
            image[:, cut] = product(
                (f_high[:, cut], f_low[:, cut]), (plane_high[...], plane_low[...]), NN
            ) + (local_pot - energy[:, 0:1]) * field[:, cut]

    def across_planes(turn, field, image, c):
        def group(i, carry):
            rows = pl.ds(pl.multiple_of(i * 8, 8), 8)
            grid = [
                ref[rows, z * PLANE : (z + 1) * PLANE]
                for ref in (faces.at[turn, 0], field, faces.at[turn, 1])
                for z in range(HALO)
            ]
            for z in range(HALO):
                cut = slice(z * PLANE, (z + 1) * PLANE)
                value = image[rows, cut]
                for d in range(1, 7):
                    value += (-KINETIC * COEF[d]) * (grid[HALO + z - d] + grid[HALO + z + d])
                image[rows, cut] = value
            return carry

        lax.fori_loop(c * chunk // 8, (c + 1) * chunk // 8, group, 0)

    def start_sum(turn):
        return [
            send(
                part.at[turn, pl.ds(pl.multiple_of(peers[k] * 8, 8), 8)],
                pieces.at[turn, k],
                sum_send.at[turn, k],
                sum_recv.at[turn, k],
                {"dom": peers[k]},
            )
            for k in range(1, slabs)
        ]

    def share_sum(turn, copies):
        mine = pl.ds(pl.multiple_of(slab * 8, 8), 8)
        value = part[turn, mine, :]
        for k in range(1, slabs):
            copies[k - 1].wait_recv()
            value += pieces[turn, k]
        summed[turn] = value
        shared = [
            send(
                summed.at[turn],
                totals.at[turn, mine],
                all_send.at[turn, k],
                all_recv.at[turn, k],
                {"dom": peers[k]},
            )
            for k in range(1, slabs)
        ]
        totals[turn, mine, :] = value
        return shared

    def finish_sum(shared):
        for copy in shared:
            copy.wait_recv()

    lane = lax.broadcasted_iota(jnp.int32, (bands, 128), 1)

    def correlate(rows):
        return product((f_high[...], f_low[...]), (w_high[rows, :], w_low[rows, :]), NT)

    def back(coefficients):
        return product(parts_of(coefficients), (w_high[...], w_low[...]), NN)

    pair = slice(every, every + 128)

    def pair_part(q, block):
        rows = slice(q * bands, (q + 2) * bands)
        both = product(
            (w_high[rows, :], w_low[rows, :]), (w_high[pair, :], w_low[pair, :]), NT
        )
        for i in range(2):
            mine = both[i * bands : (i + 1) * bands]
            if q + i:
                mine = pltpu.roll(mine, 2 * (q + i), 1)
            at = atoms + 2 * (q + i)
            block = jnp.where((lane == at) | (lane == at + 1), mine, block)
        return block

    one_cell = lax.broadcasted_iota(jnp.int32, (PLANE, PLANE), 0)
    other_cell = lax.broadcasted_iota(jnp.int32, (PLANE, PLANE), 1)
    along_x = (one_cell - other_cell) & (NX - 1)
    along_y = ((one_cell >> 4) - (other_cell >> 4)) & (NY - 1)
    away_x = jnp.minimum(along_x, NX - along_x)
    away_y = jnp.minimum(along_y, NY - along_y)
    away = jnp.where(away_x == 0, away_y, jnp.where(away_y == 0, away_x, NX))
    matrix = jnp.where(away == 0, -KINETIC * 3.0 * COEF[0], 0.0)
    for d in range(1, 7):
        matrix = jnp.where(away == d, -KINETIC * COEF[d], matrix)
    matrix_high, matrix_low = parts_of(matrix.astype(jnp.float32))
    plane_high[...] = matrix_high
    plane_low[...] = matrix_low

    for load in loads[:8]:
        load.wait()
    rows = lax.broadcasted_iota(jnp.int32, (bands, bands), 0)
    columns = lax.broadcasted_iota(jnp.int32, (bands, bands), 1)
    energy[...] = jnp.broadcast_to(
        jnp.sum(jnp.where(rows == columns, energy_row[...], 0.0), axis=1, keepdims=True), (bands, 128)
    )
    place_fields(
        slab, slabs, cells // PLANE, atoms, radial, slope, offset, owner, site, displaced, fields
    )
    for load in loads[8:]:
        load.wait()
    hold(0, occ[...])
    hold(every, fields[...])
    hold_field(start[...])
    plane_image(start, image, range(HALO))
    hand_on(0, moving, 0)
    hand_on(0, moving, 1)
    ends = slice(every, every + 128)
    on_start = correlate(ends)
    hand_on(0, moving, 2)
    shaped = pert[...] * occ[...]
    hold_field(shaped - SHIFT * start[...])
    to_sibling.wait_recv()
    hold(bands, whole[0])
    hand_on(0, moving, 3)
    part[0, :, 0 : 2 * bands] = correlate(slice(0, 2 * bands))
    on_fields = pair_part(0, on_start)
    passed = []
    for c in range(PIECES):
        crossing[c].wait_recv()
        passed.append(
            send(
                whole.at[1, pl.ds(c * half, half)],
                whole.at[2, pl.ds(c * half, half)],
                band_send.at[PIECES + c],
                band_recv.at[PIECES + c],
                {"band": sibling},
            )
        )
        hand_on(0, moving, 4 + c)
        hold(2 * bands + c * half, whole[1, c * half : (c + 1) * half])
        if c > 0:
            passed[c - 1].wait_recv()
            hold(3 * bands + (c - 1) * half, whole[2, (c - 1) * half : c * half])
    passed[PIECES - 1].wait_recv()
    hold(4 * bands - half, whole[2, bands - half :])
    part[0, :, 2 * bands : every] = correlate(slice(2 * bands, every))
    part[0, :, every:] = pair_part(2, on_fields)
    copies = start_sum(0)
    shared = share_sum(0, copies)
    for c in range(CHUNKS):
        moving[CHUNKS + c].wait_recv()
        across_planes(0, start, image, c)
    finish_sum(shared)
    last = totals[0, :, every:]
    own_radial, own_slope = last[:, atoms : atoms + 1], last[:, atoms + 1 : atoms + 2]
    swapped = jnp.where(
        lane == atoms, own_slope, jnp.where(lane == atoms + 1, own_radial, 0.0)
    )
    of_all = jnp.concatenate(
        [last] + [pltpu.roll(last, 128 - 2 * q, 1) for q in range(1, 4)], axis=0
    )
    first = totals[0, :, 0:every] + STRENGTH * product(parts_of(swapped), parts_of(of_all), NT)
    ends_part = jnp.where(lane < atoms, last, swapped)
    projected = back(jnp.concatenate([first * (1.0 / total), -STRENGTH * ends_part], axis=1))
    early = []
    for rows in (slice(0, 3 * chunk), slice(3 * chunk, bands)):
        r0[rows] = projected[rows] - image[rows] - pert[...] * occ[rows]
        if not early:
            early = [send_face(1, r0, c) for c in range(3)]

    def dot(u, v):
        return jnp.sum(u * v, axis=1, keepdims=True)

    def apply(turn, field, image, early, between=None):
        face = list(early)
        hold_field(field[...])
        on_all = correlate(slice(0, every + 128))
        part[turn, :, 0:every] = on_all[:, 0:every]
        part[turn, :, every:] = jnp.where(
            lane == atoms, dot(r0[...], field[...]), on_all[:, every:]
        )
        copies = start_sum(turn)
        face += [send_face(turn, field, c, False) for c in range(3, CHUNKS)]

        @pl.when(band % 2 == EAGER)
        def _():
            for copy in face[3:]:
                copy.start()

        @pl.when(band % 2 != EAGER)
        def _():
            for copy in face[3:DEPTH]:
                copy.start()

        plane_image(field, image, range(HALO))
        handed = []
        for c in range(CHUNKS):
            face[c].wait_recv()
            handed.append(hand_over(turn, c))
            if c + DEPTH < CHUNKS:

                @pl.when(band % 2 != EAGER)
                def _():
                    face[c + DEPTH].start()

            if c == SUM_AT:
                shared = share_sum(turn, copies)
            if c >= 4:
                handed[c - 4].wait_recv()
                across_planes(turn, field, image, c - 4)
        finish_sum(shared)
        if between is not None:
            for c in range(CHUNKS - 4, CHUNKS):
                handed[c].wait_recv()
                across_planes(turn, field, image, c)
            between(totals[turn, :, every + atoms : every + atoms + 1])
        last = totals[turn, :, every:]
        coefficients = jnp.concatenate(
            [
                totals[turn, :, 0:every] * (SHIFT / total),
                jnp.where(lane < atoms, STRENGTH * last, 0.0),
            ],
            axis=1,
        )
        image[...] += back(coefficients)
        if between is None:
            ahead.extend(send_face(turn + 1, image, c) for c in range(3))
            for c in range(CHUNKS - 4, CHUNKS):
                handed[c].wait_recv()
                across_planes(turn, field, image, c)
        return last[:, atoms : atoms + 1], coefficients

    ahead = []
    norm, _ = apply(1, r0, w0, early)
    eye = jnp.where(
        lax.broadcasted_iota(jnp.int32, (128, 128), 0)
        == lax.broadcasted_iota(jnp.int32, (128, 128), 1),
        1.0,
        0.0,
    ).astype(jnp.float32)
    last_copies = []

    def send_scalars(curve):
        alpha = norm / curve
        later = r0[...] - alpha * w0[...]
        three = jnp.where(
            lane == 0,
            dot(later, later),
            jnp.where(
                lane == 1,
                dot(later, w0[...] - alpha * image[...]),
                jnp.where(lane == 2, dot(later, w0[...]), 0.0),
            ),
        )
        three = jnp.concatenate([three, jnp.zeros((128 - bands, 128), jnp.float32)], axis=0)
        last_part[...] = lax.dot_general(
            eye[0:8], three, NT, precision=HIGH, preferred_element_type=jnp.float32
        )
        last_copies.extend(
            send(last_part, last_in.at[k], last_send.at[k], last_recv.at[k], {"dom": peers[k]})
            for k in range(1, slabs)
        )

    curve, coefficients = apply(2, w0, image, ahead, send_scalars)
    alpha = norm / curve
    on_occupied = dot(totals[1] - alpha * totals[2], coefficients)
    value = last_part[...]
    for k in range(1, slabs):
        last_copies[k - 1].wait_recv()
        value += last_in[k]
    three = lax.dot_general(
        eye[0:bands], value, NT, precision=HIGH, preferred_element_type=jnp.float32
    )
    new, cross = three[:, 0:1], three[:, 2:3]
    bend = three[:, 1:2] - alpha * on_occupied
    ratio = new / norm
    step = new / (bend + ratio * (2.0 * cross + ratio * curve))
    weights[...] = jnp.where(
        lane == 0, alpha + step * (1.0 + ratio), jnp.where(lane == 1, step * alpha, 0.0)
    )
    for copy in pending:
        copy.wait_send()


def finish_kernel(start, r0, w0, z0, weights, answer, residual, held, sems):
    bands = start.shape[0]
    size = bands // FINISH
    copies = []
    for c in range(FINISH):
        rows = pl.ds(c * size, size)
        first, second = weights[rows, 0:1], weights[rows, 1:2]
        held[0, rows] = start[rows] + first * r0[rows] - second * w0[rows]
        held[1, rows] = r0[rows] - first * w0[rows] + second * z0[rows]
        for i, out in enumerate((answer, residual)):
            copy = pltpu.make_async_copy(held.at[i, rows], out.at[0, rows], sems.at[i, c])
            copy.start()
            copies.append(copy)
    for copy in copies:
        copy.wait()


def fused(
    occupied,
    start_guess,
    potential,
    perturbation,
    energy,
    beta_radial,
    beta_slope,
    offset,
    owner,
    site,
    displaced,
):
    slabs = lax.axis_size("dom")
    atoms = owner.shape[0]
    bands, cells = occupied.shape
    every = 4 * bands
    rows = every + 128
    f32, bf16, i32 = jnp.float32, jnp.bfloat16, jnp.int32
    vmem = pl.BlockSpec(memory_space=pltpu.VMEM)
    hbm = pl.BlockSpec(memory_space=pltpu.HBM)
    out = jax.ShapeDtypeStruct((bands, cells), f32)
    dma = pltpu.SemaphoreType.DMA
    points = offset.shape[1]
    state = pl.pallas_call(
        functools.partial(fused_kernel, atoms, slabs),
        out_shape=(out, out, out, out, jax.ShapeDtypeStruct((bands, 128), f32)),
        in_specs=[hbm] * 10 + [pl.BlockSpec(memory_space=pltpu.SMEM)],
        out_specs=(vmem,) * 5,
        scratch_shapes=[
            pltpu.VMEM((bands, cells), f32),
            pltpu.VMEM((cells // 128, 128), f32),
            pltpu.VMEM((1, cells), f32),
            pltpu.VMEM((1, bands), f32),
            pltpu.VMEM((1, points), f32),
            pltpu.VMEM((1, points), f32),
            pltpu.VMEM((3, points), i32),
            pltpu.VMEM((1, atoms), i32),
            pltpu.VMEM((3, atoms), i32),
            pltpu.VMEM((bands, 128), f32),
            pltpu.VMEM((128, cells), f32),
            pltpu.VMEM((PLANE, PLANE), bf16),
            pltpu.VMEM((PLANE, PLANE), bf16),
            pltpu.VMEM((3, bands, cells), f32),
            pltpu.VMEM((rows, cells), bf16),
            pltpu.VMEM((rows, cells), bf16),
            pltpu.VMEM((bands, cells), bf16),
            pltpu.VMEM((bands, cells), bf16),
            pltpu.VMEM((3, 2, bands, cells), f32),
            pltpu.VMEM((3, bands, rows), f32),
            pltpu.VMEM((3, slabs, 8, rows), f32),
            pltpu.VMEM((3, 8, rows), f32),
            pltpu.VMEM((3, bands, rows), f32),
            pltpu.VMEM((8, 128), f32),
            pltpu.VMEM((slabs, 8, 128), f32),
            dma((2 * PIECES + 1,)),
            dma((2 * PIECES + 1,)),
            dma((3, CHUNKS)),
            dma((3, CHUNKS)),
            dma((3, CHUNKS)),
            dma((3, CHUNKS)),
            dma((3, slabs)),
            dma((3, slabs)),
            dma((3, slabs)),
            dma((3, slabs)),
            dma((slabs,)),
            dma((slabs,)),
            dma((10,)),
        ],
        compiler_params=pltpu.CompilerParams(
            collective_id=0, has_side_effects=True, vmem_limit_bytes=40 * 1024 * 1024
        ),
    )(
        *(
            pltpu.with_memory_space_constraint(x, pltpu.HBM)
            for x in (
                occupied,
                start_guess[0],
                potential.reshape(cells // 128, 128),
                perturbation,
                energy[None, :],
                beta_radial[None, :],
                beta_slope[None, :],
                offset,
                owner[None, :],
                site,
            )
        ),
        displaced,
    )
    final = jax.ShapeDtypeStruct((1, bands, cells), f32)
    return pl.pallas_call(
        finish_kernel,
        out_shape=(final, final),
        in_specs=[vmem] * 5,
        out_specs=(hbm, hbm),
        scratch_shapes=[pltpu.VMEM((2, bands, cells), f32), dma((2, FINISH))],
        compiler_params=pltpu.CompilerParams(vmem_limit_bytes=16 * 1024 * 1024),
    )(*state)


def local(
    occupied,
    start_guess,
    potential,
    perturbation,
    band_energy,
    beta_radial,
    beta_slope,
    atom_owner,
    atom_site,
    sphere_offset,
    displaced,
):
    slabs = lax.axis_size("dom")
    bands, cells = start_guess.shape[1:]
    atoms = atom_owner.shape[0]
    fits = bands == 8 * slabs and lax.axis_size("band") == 4 and atoms % 16 == 0 and atoms <= 112
    if fits and cells == HALO * PLANE:
        return fused(
            occupied,
            start_guess,
            potential,
            perturbation,
            band_energy,
            beta_radial,
            beta_slope,
            sphere_offset,
            atom_owner,
            atom_site,
            displaced,
        )
    fields = atom_fields(
        slabs, cells, beta_radial, beta_slope, sphere_offset, atom_owner, atom_site, displaced
    )
    answer, residual = plain(
        occupied,
        start_guess[0],
        potential[None, :],
        perturbation,
        band_energy[:, None],
        fields[:atoms],
        fields[atoms : atoms + 8],
        jnp.asarray(plane_matrix()),
    )
    return answer[None], residual[None]


def solution(mesh):
    return jax.shard_map(
        local,
        mesh=mesh,
        in_specs=(
            P("band", "dom"),
            P(None, "band", "dom"),
            P("dom"),
            P(None, "dom"),
            P("band"),
            P(),
            P(),
            P(),
            P(),
            P(),
            P(),
        ),
        out_specs=(P(None, "band", "dom"), P(None, "band", "dom")),
        check_vma=False,
    )
```

```python
import functools
import numpy as np
import jax
import jax.numpy as jnp
from jax import lax
from jax.experimental import pallas as pl
from jax.experimental.pallas import tpu as pltpu
from jax.sharding import PartitionSpec as P

NY = 16
NX = 16
PLANE = NY * NX
HALO = 6
CHUNKS = 8
SUM_AT = 2
FINISH = 4
PIECES = 4
EAGER = 0
DEPTH = 5
RAD = 5

COEF = (
    -5369.0 / 1800.0,
    12.0 / 7.0,
    -15.0 / 56.0,
    10.0 / 189.0,
    -1.0 / 112.0,
    2.0 / 825.0,
    -1.0 / 1386.0,
)
KINETIC = 2.0
SHIFT = 20.0
STRENGTH = 10.0
HIGH = lax.Precision.HIGHEST


def plane_matrix():
    full = np.zeros((PLANE, PLANE), np.float64)
    for y in range(NY):
        for x in range(NX):
            at = y * NX + x
            full[at, at] += 3.0 * COEF[0]
            for d in range(1, 7):
                for s in (d, -d):
                    full[((y + s) % NY) * NX + x, at] += COEF[d]
                    full[y * NX + (x + s) % NX, at] += COEF[d]
    return (-KINETIC * full).astype(np.float32)


def fields_kernel(slabs, depth, radial, slope, offset, owner, site, displaced, out, padded):
    atoms = owner.shape[0]
    planes = slabs * depth
    points = offset.shape[1]
    slab = lax.axis_index("dom")
    rows = lax.broadcasted_iota(jnp.int32, (16, points), 0)
    along_z = rows == offset[0:1, :] + RAD
    in_plane = (offset[1:2, :] & (NY - 1)) * NX + (offset[2:3, :] & (NX - 1))
    hot = jnp.where(
        lax.broadcasted_iota(jnp.int32, (PLANE, points), 0) == in_plane, 1.0, 0.0
    ).astype(jnp.float32)
    left = jnp.concatenate(
        [jnp.where(along_z, radial[...], 0.0), jnp.where(along_z, slope[...], 0.0)], axis=0
    )
    template = lax.dot_general(
        left, hot, (((1,), (1,)), ((), ())), precision=HIGH, preferred_element_type=jnp.float32
    )
    padded[...] = jnp.zeros_like(padded)
    for which in range(2):
        part = template[16 * which : 16 * which + 16]
        padded[which, 0:16, :] = part
        padded[which, planes : planes + 16, :] = part
    column = lax.broadcasted_iota(jnp.int32, (8, PLANE), 1) & (NX - 1)

    def shifted(which, a):
        z = lax.rem(slab * depth + RAD + 2 * planes - owner[a] * depth - site[0, a], planes)
        x = site[2, a]
        turn = site[1, a] * NX + x
        start = pl.multiple_of(lax.div(z, 8) * 8, 8)
        block = pltpu.roll(padded[which, pl.ds(start, 16), :], lax.rem(16 - lax.rem(z, 8), 16), 0)[0:8]
        first = pltpu.roll(block, turn, 1)
        second = pltpu.roll(block, lax.rem(turn + PLANE - NX, PLANE), 1)
        return jnp.where(column >= x, first, second)

    out[atoms:, :] = jnp.zeros((out.shape[0] - atoms, out.shape[1]), jnp.float32)
    for row in range(atoms + 2):
        field = shifted(0, row) if row < atoms else shifted(row - atoms, displaced[0])
        for z in range(depth):
            out[row : row + 1, z * PLANE : (z + 1) * PLANE] = field[z : z + 1]


def place_fields(slab, slabs, depth, atoms, radial, slope, offset, owner, site, displaced, fields):
    planes = slabs * depth
    points = offset.shape[1]
    count = atoms + 8
    rows = lax.broadcasted_iota(jnp.int32, (16, points), 0)
    along_z = rows == offset[0:1, :] + RAD
    in_plane = (offset[1:2, :] & (NY - 1)) * NX + (offset[2:3, :] & (NX - 1))
    hot = jnp.where(
        lax.broadcasted_iota(jnp.int32, (PLANE, points), 0) == in_plane, 1.0, 0.0
    ).astype(jnp.float32)
    left = jnp.concatenate(
        [jnp.where(along_z, radial[...], 0.0), jnp.where(along_z, slope[...], 0.0)], axis=0
    )
    template = lax.dot_general(
        left, hot, (((1,), (1,)), ((), ())), precision=HIGH, preferred_element_type=jnp.float32
    )
    row = lax.broadcasted_iota(jnp.int32, (count, atoms), 0)
    atom = lax.broadcasted_iota(jnp.int32, (count, atoms), 1)
    chosen = atom == jnp.where(row < atoms, row, displaced[0])

    def column(values):
        return jnp.sum(jnp.where(chosen, values, 0), axis=1, keepdims=True)

    centre = column(owner[...]) * depth + column(site[0:1, :])
    turn_y, turn_x = column(site[1:2, :]), column(site[2:3, :])
    row = lax.broadcasted_iota(jnp.int32, (count, 32), 0)
    lane = lax.broadcasted_iota(jnp.int32, (count, 32), 1)
    picks = []
    for z in range(depth):
        at = slab * depth + (z + RAD) - centre
        at = jnp.where(at < 0, at + planes, jnp.where(at >= planes, at - planes, at))
        at = jnp.where(at < 16, at, -32)
        pick = lane == at + jnp.where(row == atoms + 1, 16, 0)
        picks.append(jnp.where(pick & (row < atoms + 2), 1.0, 0.0).astype(jnp.float32))
    value = lax.dot_general(
        jnp.concatenate(picks, axis=0),
        template,
        (((1,), (0,)), ((), ())),
        precision=HIGH,
        preferred_element_type=jnp.float32,
    )
    x = lax.broadcasted_iota(jnp.int32, (count, PLANE), 1) & (NX - 1)
    wide_x = jnp.broadcast_to(turn_x, (count, PLANE))
    wide_y = jnp.broadcast_to(turn_y, (count, PLANE))
    fields[atoms:, :] = jnp.zeros((fields.shape[0] - atoms, fields.shape[1]), jnp.float32)
    for z in range(depth):
        block = value[z * count : (z + 1) * count]
        for d in (1, 2, 4, 8):
            near, far = pltpu.roll(block, d, 1), pltpu.roll(block, PLANE + d - NX, 1)
            block = jnp.where((wide_x & d) != 0, jnp.where(x >= d, near, far), block)
        for d in (1, 2, 4, 8):
            block = jnp.where((wide_y & d) != 0, pltpu.roll(block, d * NX, 1), block)
        fields[0:count, z * PLANE : (z + 1) * PLANE] = block


def atom_fields(slabs, cells, beta_radial, beta_slope, offset, owner, site, displaced):
    atoms = owner.shape[0]
    depth = cells // PLANE
    vmem = pl.BlockSpec(memory_space=pltpu.VMEM)
    smem = pl.BlockSpec(memory_space=pltpu.SMEM)
    return pl.pallas_call(
        functools.partial(fields_kernel, slabs, depth),
        out_shape=jax.ShapeDtypeStruct((max(128, atoms + 16), cells), jnp.float32),
        in_specs=[vmem, vmem, vmem, smem, smem, smem],
        out_specs=vmem,
        scratch_shapes=[pltpu.VMEM((2, slabs * depth + 16, PLANE), jnp.float32)],
        compiler_params=pltpu.CompilerParams(vmem_limit_bytes=16 * 1024 * 1024),
    )(beta_radial[None, :], beta_slope[None, :], offset, owner, site, displaced)


def times(a, b, dims):
    return lax.dot_general(a, b, (dims, ((), ())), precision=HIGH, preferred_element_type=jnp.float32)


def plain(occupied, start, potential, perturbation, energy, beta, pair, in_plane):
    slabs = lax.axis_size("dom")
    bands, cells = start.shape
    depth = cells // PLANE
    total = cells * slabs
    whole = lax.all_gather(occupied, "band", axis=0, tiled=True)
    every = whole.shape[0]
    up = [(i, (i + 1) % slabs) for i in range(slabs)]
    down = [(j, i) for i, j in up]

    def local_part(field):
        before = lax.ppermute(field, "dom", up)
        after = lax.ppermute(field, "dom", down)
        grid = jnp.concatenate([before, field, after], axis=1)
        image = times(field.reshape(bands * depth, PLANE), in_plane, ((1,), (0,))).reshape(bands, cells)
        for d in range(1, 7):
            low = (depth - d) * PLANE
            high = (depth + d) * PLANE
            image += (-KINETIC * COEF[d]) * (grid[:, low : low + cells] + grid[:, high : high + cells])
        return image + (potential - energy) * field

    def correlate(field):
        return jnp.concatenate(
            [times(field, whole, ((1,), (1,))), times(field, beta, ((1,), (1,)))], axis=1
        )

    def operator(field, total_correlation):
        return (
            local_part(field)
            + (SHIFT / total) * times(total_correlation[:, :every], whole, ((1,), (0,)))
            + STRENGTH * times(total_correlation[:, every:], beta, ((1,), (0,)))
        )

    def dot(u, v):
        return jnp.sum(u * v, axis=1, keepdims=True)

    shaped = perturbation * occupied
    first, on_atoms, own, of_all = lax.psum(
        (
            times(shaped - SHIFT * start, whole, ((1,), (1,))),
            times(start, beta, ((1,), (1,))),
            times(occupied, pair, ((1,), (1,))),
            times(pair, whole, ((1,), (1,))),
        ),
        "dom",
    )
    own_radial, own_slope = own[:, 0:1], own[:, 1:2]
    first = first + STRENGTH * (own_radial * of_all[1:2] + own_slope * of_all[0:1])
    residual = (
        times(first * (1.0 / total), whole, ((1,), (0,)))
        - STRENGTH * times(on_atoms, beta, ((1,), (0,)))
        - local_part(start)
        - shaped
        - STRENGTH * (own_radial * pair[1:2] + own_slope * pair[0:1])
    )
    correlation, norm = lax.psum((correlate(residual), dot(residual, residual)), "dom")
    image = operator(residual, correlation)
    correlation, curve = lax.psum((correlate(image), dot(residual, image)), "dom")
    alpha = norm / curve
    again = operator(image, correlation)
    later = residual - alpha * image
    later_image = image - alpha * again
    new, bend, cross = lax.psum((dot(later, later), dot(later, later_image), dot(later, image)), "dom")
    ratio = new / norm
    step = new / (bend + ratio * (2.0 * cross + ratio * curve))
    answer = start + alpha * residual + step * (later + ratio * residual)
    return answer, later - step * (later_image + ratio * image)


NT = (((1,), (1,)), ((), ()))
NN = (((1,), (0,)), ((), ()))
MESH = pl.DeviceIdType.MESH


def parts_of(x):
    high = x.astype(jnp.bfloat16)
    return high, (x - high.astype(jnp.float32)).astype(jnp.bfloat16)


def product(a, b, dims):
    def one(u, v):
        return lax.dot_general(u, v, dims, preferred_element_type=jnp.float32)

    rows = a[0].shape[0]
    both = one(jnp.concatenate(a, axis=0), b[0])
    return both[:rows] + (one(a[0], b[1]) + both[rows:])


def fused_kernel(
    atoms,
    slabs,
    occ_in,
    start_in,
    pot_in,
    pert_in,
    energy_in,
    radial_in,
    slope_in,
    offset_in,
    owner_in,
    site_in,
    displaced,
    start,
    r0,
    w0,
    image,
    weights,
    occ,
    pot,
    pert,
    energy_row,
    radial,
    slope,
    offset,
    owner,
    site,
    energy,
    fields,
    plane_high,
    plane_low,
    whole,
    w_high,
    w_low,
    f_high,
    f_low,
    faces,
    part,
    pieces,
    summed,
    totals,
    last_part,
    last_in,
    band_send,
    band_recv,
    face_send,
    face_recv,
    hand_send,
    hand_recv,
    sum_send,
    sum_recv,
    all_send,
    all_recv,
    last_send,
    last_recv,
    local_sem,
):
    bands, cells = occ.shape
    every = 4 * bands
    total = cells * slabs
    band = lax.axis_index("band")
    slab = lax.axis_index("dom")
    sibling = band + 1 - 2 * (band % 2)
    across = (band + 2) % 4
    barrier = pltpu.get_barrier_semaphore()
    pl.semaphore_signal(barrier, inc=1, device_id={"band": sibling}, device_id_type=MESH)
    pl.semaphore_signal(barrier, inc=1, device_id={"band": across}, device_id_type=MESH)
    peers = [(slab + k) % slabs for k in range(slabs)]
    for k in range(1, slabs):
        pl.semaphore_signal(barrier, inc=1, device_id={"dom": peers[k]}, device_id_type=MESH)
    loads = [
        pltpu.make_async_copy(src, dst, local_sem.at[i])
        for i, (src, dst) in enumerate(
            (
                (offset_in, offset),
                (radial_in, radial),
                (slope_in, slope),
                (owner_in, owner),
                (site_in, site),
                (energy_in, energy_row),
                (pot_in, pot),
                (pert_in, pert),
                (start_in, start),
                (occ_in, occ),
            )
        )
    ]
    for load in loads:
        load.start()
    pl.semaphore_wait(barrier, slabs + 1)

    pending = []

    def send(src, dst, send_sem, recv_sem, device, begin=True):
        copy = pltpu.make_async_remote_copy(
            src_ref=src,
            dst_ref=dst,
            send_sem=send_sem,
            recv_sem=recv_sem,
            device_id=device,
            device_id_type=MESH,
        )
        if begin:
            copy.start()
        pending.append(copy)
        return copy

    chunk = bands // CHUNKS
    side = slab % 2
    beside = slab + 1 - 2 * side
    beyond = (slab + slabs + 2 - 4 * side) % slabs

    def send_face(turn, field, c, begin=True):
        return send(
            field.at[pl.ds(c * chunk, chunk)],
            faces.at[turn, side, pl.ds(c * chunk, chunk)],
            face_send.at[turn, c],
            face_recv.at[turn, c],
            {"dom": beside},
            begin,
        )

    def hand_over(turn, c):
        return send(
            faces.at[turn, 1 - side, pl.ds(c * chunk, chunk)],
            faces.at[turn, side, pl.ds(c * chunk, chunk)],
            hand_send.at[turn, c],
            hand_recv.at[turn, c],
            {"dom": beyond},
        )

    def hand_on(turn, copies, c):
        copies[c].wait_recv()
        copies.append(hand_over(turn, c))

    half = bands // PIECES
    crossing = [
        send(
            occ_in.at[pl.ds(c * half, half)],
            whole.at[1, pl.ds(c * half, half)],
            band_send.at[c],
            band_recv.at[c],
            {"band": across},
        )
        for c in range(PIECES)
    ]
    to_sibling = send(occ_in, whole.at[0], band_send.at[2 * PIECES], band_recv.at[2 * PIECES], {"band": sibling})
    moving = [send_face(0, start_in, c) for c in range(CHUNKS)]

    def hold(row, block):
        high, low = parts_of(block)
        w_high[row : row + block.shape[0], :] = high
        w_low[row : row + block.shape[0], :] = low

    def hold_field(block):
        high, low = parts_of(block)
        f_high[...] = high
        f_low[...] = low

    def plane_image(field, image, planes):
        for z in planes:
            cut = slice(z * PLANE, (z + 1) * PLANE)
            local_pot = jnp.concatenate(
                [pot[i : i + 1] for i in range(z * PLANE // 128, (z + 1) * PLANE // 128)], axis=1
            )
            image[:, cut] = product(
                (f_high[:, cut], f_low[:, cut]), (plane_high[...], plane_low[...]), NN
            ) + (local_pot - energy[:, 0:1]) * field[:, cut]

    def across_planes(turn, field, image, c):
        def group(i, carry):
            rows = pl.ds(pl.multiple_of(i * 8, 8), 8)
            grid = [
                ref[rows, z * PLANE : (z + 1) * PLANE]
                for ref in (faces.at[turn, 0], field, faces.at[turn, 1])
                for z in range(HALO)
            ]
            for z in range(HALO):
                cut = slice(z * PLANE, (z + 1) * PLANE)
                value = image[rows, cut]
                for d in range(1, 7):
                    value += (-KINETIC * COEF[d]) * (grid[HALO + z - d] + grid[HALO + z + d])
                image[rows, cut] = value
            return carry

        lax.fori_loop(c * chunk // 8, (c + 1) * chunk // 8, group, 0)

    def start_sum(turn):
        return [
            send(
                part.at[turn, pl.ds(pl.multiple_of(peers[k] * 8, 8), 8)],
                pieces.at[turn, k],
                sum_send.at[turn, k],
                sum_recv.at[turn, k],
                {"dom": peers[k]},
            )
            for k in range(1, slabs)
        ]

    def share_sum(turn, copies):
        mine = pl.ds(pl.multiple_of(slab * 8, 8), 8)
        value = part[turn, mine, :]
        for k in range(1, slabs):
            copies[k - 1].wait_recv()
            value += pieces[turn, k]
        summed[turn] = value
        shared = [
            send(
                summed.at[turn],
                totals.at[turn, mine],
                all_send.at[turn, k],
                all_recv.at[turn, k],
                {"dom": peers[k]},
            )
            for k in range(1, slabs)
        ]
        totals[turn, mine, :] = value
        return shared

    def finish_sum(shared):
        for copy in shared:
            copy.wait_recv()

    lane = lax.broadcasted_iota(jnp.int32, (bands, 128), 1)

    def correlate(rows):
        return product((f_high[...], f_low[...]), (w_high[rows, :], w_low[rows, :]), NT)

    def back(coefficients):
        return product(parts_of(coefficients), (w_high[...], w_low[...]), NN)

    pair = slice(every, every + 128)

    def pair_part(q, block):
        rows = slice(q * bands, (q + 2) * bands)
        both = product(
            (w_high[rows, :], w_low[rows, :]), (w_high[pair, :], w_low[pair, :]), NT
        )
        for i in range(2):
            mine = both[i * bands : (i + 1) * bands]
            if q + i:
                mine = pltpu.roll(mine, 2 * (q + i), 1)
            at = atoms + 2 * (q + i)
            block = jnp.where((lane == at) | (lane == at + 1), mine, block)
        return block

    one_cell = lax.broadcasted_iota(jnp.int32, (PLANE, PLANE), 0)
    other_cell = lax.broadcasted_iota(jnp.int32, (PLANE, PLANE), 1)
    along_x = (one_cell - other_cell) & (NX - 1)
    along_y = ((one_cell >> 4) - (other_cell >> 4)) & (NY - 1)
    away_x = jnp.minimum(along_x, NX - along_x)
    away_y = jnp.minimum(along_y, NY - along_y)
    away = jnp.where(away_x == 0, away_y, jnp.where(away_y == 0, away_x, NX))
    matrix = jnp.where(away == 0, -KINETIC * 3.0 * COEF[0], 0.0)
    for d in range(1, 7):
        matrix = jnp.where(away == d, -KINETIC * COEF[d], matrix)
    matrix_high, matrix_low = parts_of(matrix.astype(jnp.float32))
    plane_high[...] = matrix_high
    plane_low[...] = matrix_low

    for load in loads[:8]:
        load.wait()
    rows = lax.broadcasted_iota(jnp.int32, (bands, bands), 0)
    columns = lax.broadcasted_iota(jnp.int32, (bands, bands), 1)
    energy[...] = jnp.broadcast_to(
        jnp.sum(jnp.where(rows == columns, energy_row[...], 0.0), axis=1, keepdims=True), (bands, 128)
    )
    place_fields(
        slab, slabs, cells // PLANE, atoms, radial, slope, offset, owner, site, displaced, fields
    )
    for load in loads[8:]:
        load.wait()
    hold(0, occ[...])
    hold(every, fields[...])
    hold_field(start[...])
    plane_image(start, image, range(HALO))
    hand_on(0, moving, 0)
    hand_on(0, moving, 1)
    ends = slice(every, every + 128)
    on_start = correlate(ends)
    hand_on(0, moving, 2)
    shaped = pert[...] * occ[...]
    hold_field(shaped - SHIFT * start[...])
    to_sibling.wait_recv()
    hold(bands, whole[0])
    hand_on(0, moving, 3)
    part[0, :, 0 : 2 * bands] = correlate(slice(0, 2 * bands))
    on_fields = pair_part(0, on_start)
    passed = []
    for c in range(PIECES):
        crossing[c].wait_recv()
        passed.append(
            send(
                whole.at[1, pl.ds(c * half, half)],
                whole.at[2, pl.ds(c * half, half)],
                band_send.at[PIECES + c],
                band_recv.at[PIECES + c],
                {"band": sibling},
            )
        )
        hand_on(0, moving, 4 + c)
        hold(2 * bands + c * half, whole[1, c * half : (c + 1) * half])
        if c > 0:
            passed[c - 1].wait_recv()
            hold(3 * bands + (c - 1) * half, whole[2, (c - 1) * half : c * half])
    passed[PIECES - 1].wait_recv()
    hold(4 * bands - half, whole[2, bands - half :])
    part[0, :, 2 * bands : every] = correlate(slice(2 * bands, every))
    part[0, :, every:] = pair_part(2, on_fields)
    copies = start_sum(0)
    shared = share_sum(0, copies)
    for c in range(CHUNKS):
        moving[CHUNKS + c].wait_recv()
        across_planes(0, start, image, c)
    finish_sum(shared)
    last = totals[0, :, every:]
    own_radial, own_slope = last[:, atoms : atoms + 1], last[:, atoms + 1 : atoms + 2]
    swapped = jnp.where(
        lane == atoms, own_slope, jnp.where(lane == atoms + 1, own_radial, 0.0)
    )
    of_all = jnp.concatenate(
        [last] + [pltpu.roll(last, 128 - 2 * q, 1) for q in range(1, 4)], axis=0
    )
    first = totals[0, :, 0:every] + STRENGTH * product(parts_of(swapped), parts_of(of_all), NT)
    ends_part = jnp.where(lane < atoms, last, swapped)
    projected = back(jnp.concatenate([first * (1.0 / total), -STRENGTH * ends_part], axis=1))
    early = []
    for rows in (slice(0, 3 * chunk), slice(3 * chunk, bands)):
        r0[rows] = projected[rows] - image[rows] - pert[...] * occ[rows]
        if not early:
            early = [send_face(1, r0, c) for c in range(3)]

    def dot(u, v):
        return jnp.sum(u * v, axis=1, keepdims=True)

    def apply(turn, field, image, early, between=None):
        face = list(early)
        hold_field(field[...])
        on_all = correlate(slice(0, every + 128))
        part[turn, :, 0:every] = on_all[:, 0:every]
        part[turn, :, every:] = jnp.where(
            lane == atoms, dot(r0[...], field[...]), on_all[:, every:]
        )
        copies = start_sum(turn)
        face += [send_face(turn, field, c, False) for c in range(3, CHUNKS)]

        @pl.when(band % 2 == EAGER)
        def _():
            for copy in face[3:]:
                copy.start()

        @pl.when(band % 2 != EAGER)
        def _():
            for copy in face[3:DEPTH]:
                copy.start()

        plane_image(field, image, range(HALO))
        handed = []
        for c in range(CHUNKS):
            face[c].wait_recv()
            handed.append(hand_over(turn, c))
            if c + DEPTH < CHUNKS:

                @pl.when(band % 2 != EAGER)
                def _():
                    face[c + DEPTH].start()

            if c == SUM_AT:
                shared = share_sum(turn, copies)
            if c >= 4:
                handed[c - 4].wait_recv()
                across_planes(turn, field, image, c - 4)
        handed[CHUNKS - 4].wait_recv()
        across_planes(turn, field, image, CHUNKS - 4)
        finish_sum(shared)
        if between is not None:
            for c in range(CHUNKS - 3, CHUNKS):
                handed[c].wait_recv()
                across_planes(turn, field, image, c)
            between(totals[turn, :, every + atoms : every + atoms + 1])
        last = totals[turn, :, every:]
        coefficients = jnp.concatenate(
            [
                totals[turn, :, 0:every] * (SHIFT / total),
                jnp.where(lane < atoms, STRENGTH * last, 0.0),
            ],
            axis=1,
        )
        image[...] += back(coefficients)
        if between is None:
            ahead.extend(send_face(turn + 1, image, c) for c in range(3))
            for c in range(CHUNKS - 3, CHUNKS):
                handed[c].wait_recv()
                across_planes(turn, field, image, c)
        return last[:, atoms : atoms + 1], coefficients

    ahead = []
    norm, _ = apply(1, r0, w0, early)
    eye = jnp.where(
        lax.broadcasted_iota(jnp.int32, (128, 128), 0)
        == lax.broadcasted_iota(jnp.int32, (128, 128), 1),
        1.0,
        0.0,
    ).astype(jnp.float32)
    last_copies = []

    def send_scalars(curve):
        alpha = norm / curve
        later = r0[...] - alpha * w0[...]
        three = jnp.where(
            lane == 0,
            dot(later, later),
            jnp.where(
                lane == 1,
                dot(later, w0[...] - alpha * image[...]),
                jnp.where(lane == 2, dot(later, w0[...]), 0.0),
            ),
        )
        three = jnp.concatenate([three, jnp.zeros((128 - bands, 128), jnp.float32)], axis=0)
        last_part[...] = lax.dot_general(
            eye[0:8], three, NT, precision=HIGH, preferred_element_type=jnp.float32
        )
        last_copies.extend(
            send(last_part, last_in.at[k], last_send.at[k], last_recv.at[k], {"dom": peers[k]})
            for k in range(1, slabs)
        )

    curve, coefficients = apply(2, w0, image, ahead, send_scalars)
    alpha = norm / curve
    on_occupied = dot(totals[1] - alpha * totals[2], coefficients)
    value = last_part[...]
    for k in range(1, slabs):
        last_copies[k - 1].wait_recv()
        value += last_in[k]
    three = lax.dot_general(
        eye[0:bands], value, NT, precision=HIGH, preferred_element_type=jnp.float32
    )
    new, cross = three[:, 0:1], three[:, 2:3]
    bend = three[:, 1:2] - alpha * on_occupied
    ratio = new / norm
    step = new / (bend + ratio * (2.0 * cross + ratio * curve))
    weights[...] = jnp.where(
        lane == 0, alpha + step * (1.0 + ratio), jnp.where(lane == 1, step * alpha, 0.0)
    )
    for copy in pending:
        copy.wait_send()


def finish_kernel(start, r0, w0, z0, weights, answer, residual, held, sems):
    bands = start.shape[0]
    size = bands // FINISH
    copies = []
    for c in range(FINISH):
        rows = pl.ds(c * size, size)
        first, second = weights[rows, 0:1], weights[rows, 1:2]
        held[0, rows] = start[rows] + first * r0[rows] - second * w0[rows]
        held[1, rows] = r0[rows] - first * w0[rows] + second * z0[rows]
        for i, out in enumerate((answer, residual)):
            copy = pltpu.make_async_copy(held.at[i, rows], out.at[0, rows], sems.at[i, c])
            copy.start()
            copies.append(copy)
    for copy in copies:
        copy.wait()


def fused(
    occupied,
    start_guess,
    potential,
    perturbation,
    energy,
    beta_radial,
    beta_slope,
    offset,
    owner,
    site,
    displaced,
):
    slabs = lax.axis_size("dom")
    atoms = owner.shape[0]
    bands, cells = occupied.shape
    every = 4 * bands
    rows = every + 128
    f32, bf16, i32 = jnp.float32, jnp.bfloat16, jnp.int32
    vmem = pl.BlockSpec(memory_space=pltpu.VMEM)
    hbm = pl.BlockSpec(memory_space=pltpu.HBM)
    out = jax.ShapeDtypeStruct((bands, cells), f32)
    dma = pltpu.SemaphoreType.DMA
    points = offset.shape[1]
    state = pl.pallas_call(
        functools.partial(fused_kernel, atoms, slabs),
        out_shape=(out, out, out, out, jax.ShapeDtypeStruct((bands, 128), f32)),
        in_specs=[hbm] * 10 + [pl.BlockSpec(memory_space=pltpu.SMEM)],
        out_specs=(vmem,) * 5,
        scratch_shapes=[
            pltpu.VMEM((bands, cells), f32),
            pltpu.VMEM((cells // 128, 128), f32),
            pltpu.VMEM((1, cells), f32),
            pltpu.VMEM((1, bands), f32),
            pltpu.VMEM((1, points), f32),
            pltpu.VMEM((1, points), f32),
            pltpu.VMEM((3, points), i32),
            pltpu.VMEM((1, atoms), i32),
            pltpu.VMEM((3, atoms), i32),
            pltpu.VMEM((bands, 128), f32),
            pltpu.VMEM((128, cells), f32),
            pltpu.VMEM((PLANE, PLANE), bf16),
            pltpu.VMEM((PLANE, PLANE), bf16),
            pltpu.VMEM((3, bands, cells), f32),
            pltpu.VMEM((rows, cells), bf16),
            pltpu.VMEM((rows, cells), bf16),
            pltpu.VMEM((bands, cells), bf16),
            pltpu.VMEM((bands, cells), bf16),
            pltpu.VMEM((3, 2, bands, cells), f32),
            pltpu.VMEM((3, bands, rows), f32),
            pltpu.VMEM((3, slabs, 8, rows), f32),
            pltpu.VMEM((3, 8, rows), f32),
            pltpu.VMEM((3, bands, rows), f32),
            pltpu.VMEM((8, 128), f32),
            pltpu.VMEM((slabs, 8, 128), f32),
            dma((2 * PIECES + 1,)),
            dma((2 * PIECES + 1,)),
            dma((3, CHUNKS)),
            dma((3, CHUNKS)),
            dma((3, CHUNKS)),
            dma((3, CHUNKS)),
            dma((3, slabs)),
            dma((3, slabs)),
            dma((3, slabs)),
            dma((3, slabs)),
            dma((slabs,)),
            dma((slabs,)),
            dma((10,)),
        ],
        compiler_params=pltpu.CompilerParams(
            collective_id=0, has_side_effects=True, vmem_limit_bytes=40 * 1024 * 1024
        ),
    )(
        *(
            pltpu.with_memory_space_constraint(x, pltpu.HBM)
            for x in (
                occupied,
                start_guess[0],
                potential.reshape(cells // 128, 128),
                perturbation,
                energy[None, :],
                beta_radial[None, :],
                beta_slope[None, :],
                offset,
                owner[None, :],
                site,
            )
        ),
        displaced,
    )
    final = jax.ShapeDtypeStruct((1, bands, cells), f32)
    return pl.pallas_call(
        finish_kernel,
        out_shape=(final, final),
        in_specs=[vmem] * 5,
        out_specs=(hbm, hbm),
        scratch_shapes=[pltpu.VMEM((2, bands, cells), f32), dma((2, FINISH))],
        compiler_params=pltpu.CompilerParams(vmem_limit_bytes=16 * 1024 * 1024),
    )(*state)


def local(
    occupied,
    start_guess,
    potential,
    perturbation,
    band_energy,
    beta_radial,
    beta_slope,
    atom_owner,
    atom_site,
    sphere_offset,
    displaced,
):
    slabs = lax.axis_size("dom")
    bands, cells = start_guess.shape[1:]
    atoms = atom_owner.shape[0]
    fits = bands == 8 * slabs and lax.axis_size("band") == 4 and atoms % 16 == 0 and atoms <= 112
    if fits and cells == HALO * PLANE:
        return fused(
            occupied,
            start_guess,
            potential,
            perturbation,
            band_energy,
            beta_radial,
            beta_slope,
            sphere_offset,
            atom_owner,
            atom_site,
            displaced,
        )
    fields = atom_fields(
        slabs, cells, beta_radial, beta_slope, sphere_offset, atom_owner, atom_site, displaced
    )
    answer, residual = plain(
        occupied,
        start_guess[0],
        potential[None, :],
        perturbation,
        band_energy[:, None],
        fields[:atoms],
        fields[atoms : atoms + 8],
        jnp.asarray(plane_matrix()),
    )
    return answer[None], residual[None]


def solution(mesh):
    return jax.shard_map(
        local,
        mesh=mesh,
        in_specs=(
            P("band", "dom"),
            P(None, "band", "dom"),
            P("dom"),
            P(None, "dom"),
            P("band"),
            P(),
            P(),
            P(),
            P(),
            P(),
            P(),
        ),
        out_specs=(P(None, "band", "dom"), P(None, "band", "dom")),
        check_vma=False,
    )
```

```python
import functools
import numpy as np
import jax
import jax.numpy as jnp
from jax import lax
from jax.experimental import pallas as pl
from jax.experimental.pallas import tpu as pltpu
from jax.sharding import PartitionSpec as P

NY = 16
NX = 16
PLANE = NY * NX
HALO = 6
CHUNKS = 8
SUM_AT = 2
FINISH = 4
PIECES = 4
EAGER = 0
DEPTH = 5
RAD = 5

COEF = (
    -5369.0 / 1800.0,
    12.0 / 7.0,
    -15.0 / 56.0,
    10.0 / 189.0,
    -1.0 / 112.0,
    2.0 / 825.0,
    -1.0 / 1386.0,
)
KINETIC = 2.0
SHIFT = 20.0
STRENGTH = 10.0
HIGH = lax.Precision.HIGHEST


def plane_matrix():
    full = np.zeros((PLANE, PLANE), np.float64)
    for y in range(NY):
        for x in range(NX):
            at = y * NX + x
            full[at, at] += 3.0 * COEF[0]
            for d in range(1, 7):
                for s in (d, -d):
                    full[((y + s) % NY) * NX + x, at] += COEF[d]
                    full[y * NX + (x + s) % NX, at] += COEF[d]
    return (-KINETIC * full).astype(np.float32)


def fields_kernel(slabs, depth, radial, slope, offset, owner, site, displaced, out, padded):
    atoms = owner.shape[0]
    planes = slabs * depth
    points = offset.shape[1]
    slab = lax.axis_index("dom")
    rows = lax.broadcasted_iota(jnp.int32, (16, points), 0)
    along_z = rows == offset[0:1, :] + RAD
    in_plane = (offset[1:2, :] & (NY - 1)) * NX + (offset[2:3, :] & (NX - 1))
    hot = jnp.where(
        lax.broadcasted_iota(jnp.int32, (PLANE, points), 0) == in_plane, 1.0, 0.0
    ).astype(jnp.float32)
    left = jnp.concatenate(
        [jnp.where(along_z, radial[...], 0.0), jnp.where(along_z, slope[...], 0.0)], axis=0
    )
    template = lax.dot_general(
        left, hot, (((1,), (1,)), ((), ())), precision=HIGH, preferred_element_type=jnp.float32
    )
    padded[...] = jnp.zeros_like(padded)
    for which in range(2):
        part = template[16 * which : 16 * which + 16]
        padded[which, 0:16, :] = part
        padded[which, planes : planes + 16, :] = part
    column = lax.broadcasted_iota(jnp.int32, (8, PLANE), 1) & (NX - 1)

    def shifted(which, a):
        z = lax.rem(slab * depth + RAD + 2 * planes - owner[a] * depth - site[0, a], planes)
        x = site[2, a]
        turn = site[1, a] * NX + x
        start = pl.multiple_of(lax.div(z, 8) * 8, 8)
        block = pltpu.roll(padded[which, pl.ds(start, 16), :], lax.rem(16 - lax.rem(z, 8), 16), 0)[0:8]
        first = pltpu.roll(block, turn, 1)
        second = pltpu.roll(block, lax.rem(turn + PLANE - NX, PLANE), 1)
        return jnp.where(column >= x, first, second)

    out[atoms:, :] = jnp.zeros((out.shape[0] - atoms, out.shape[1]), jnp.float32)
    for row in range(atoms + 2):
        field = shifted(0, row) if row < atoms else shifted(row - atoms, displaced[0])
        for z in range(depth):
            out[row : row + 1, z * PLANE : (z + 1) * PLANE] = field[z : z + 1]


def place_fields(slab, slabs, depth, atoms, radial, slope, offset, owner, site, displaced, fields):
    planes = slabs * depth
    points = offset.shape[1]
    count = atoms + 8
    rows = lax.broadcasted_iota(jnp.int32, (16, points), 0)
    along_z = rows == offset[0:1, :] + RAD
    in_plane = (offset[1:2, :] & (NY - 1)) * NX + (offset[2:3, :] & (NX - 1))
    hot = jnp.where(
        lax.broadcasted_iota(jnp.int32, (PLANE, points), 0) == in_plane, 1.0, 0.0
    ).astype(jnp.float32)
    left = jnp.concatenate(
        [jnp.where(along_z, radial[...], 0.0), jnp.where(along_z, slope[...], 0.0)], axis=0
    )
    template = lax.dot_general(
        left, hot, (((1,), (1,)), ((), ())), precision=HIGH, preferred_element_type=jnp.float32
    )
    row = lax.broadcasted_iota(jnp.int32, (count, atoms), 0)
    atom = lax.broadcasted_iota(jnp.int32, (count, atoms), 1)
    chosen = atom == jnp.where(row < atoms, row, displaced[0])

    def column(values):
        return jnp.sum(jnp.where(chosen, values, 0), axis=1, keepdims=True)

    centre = column(owner[...]) * depth + column(site[0:1, :])
    turn_y, turn_x = column(site[1:2, :]), column(site[2:3, :])
    row = lax.broadcasted_iota(jnp.int32, (count, 32), 0)
    lane = lax.broadcasted_iota(jnp.int32, (count, 32), 1)
    picks = []
    for z in range(depth):
        at = slab * depth + (z + RAD) - centre
        at = jnp.where(at < 0, at + planes, jnp.where(at >= planes, at - planes, at))
        at = jnp.where(at < 16, at, -32)
        pick = lane == at + jnp.where(row == atoms + 1, 16, 0)
        picks.append(jnp.where(pick & (row < atoms + 2), 1.0, 0.0).astype(jnp.float32))
    value = lax.dot_general(
        jnp.concatenate(picks, axis=0),
        template,
        (((1,), (0,)), ((), ())),
        precision=HIGH,
        preferred_element_type=jnp.float32,
    )
    x = lax.broadcasted_iota(jnp.int32, (count, PLANE), 1) & (NX - 1)
    wide_x = jnp.broadcast_to(turn_x, (count, PLANE))
    wide_y = jnp.broadcast_to(turn_y, (count, PLANE))
    fields[atoms:, :] = jnp.zeros((fields.shape[0] - atoms, fields.shape[1]), jnp.float32)
    for z in range(depth):
        block = value[z * count : (z + 1) * count]
        for d in (1, 2, 4, 8):
            near, far = pltpu.roll(block, d, 1), pltpu.roll(block, PLANE + d - NX, 1)
            block = jnp.where((wide_x & d) != 0, jnp.where(x >= d, near, far), block)
        for d in (1, 2, 4, 8):
            block = jnp.where((wide_y & d) != 0, pltpu.roll(block, d * NX, 1), block)
        fields[0:count, z * PLANE : (z + 1) * PLANE] = block


def atom_fields(slabs, cells, beta_radial, beta_slope, offset, owner, site, displaced):
    atoms = owner.shape[0]
    depth = cells // PLANE
    vmem = pl.BlockSpec(memory_space=pltpu.VMEM)
    smem = pl.BlockSpec(memory_space=pltpu.SMEM)
    return pl.pallas_call(
        functools.partial(fields_kernel, slabs, depth),
        out_shape=jax.ShapeDtypeStruct((max(128, atoms + 16), cells), jnp.float32),
        in_specs=[vmem, vmem, vmem, smem, smem, smem],
        out_specs=vmem,
        scratch_shapes=[pltpu.VMEM((2, slabs * depth + 16, PLANE), jnp.float32)],
        compiler_params=pltpu.CompilerParams(vmem_limit_bytes=16 * 1024 * 1024),
    )(beta_radial[None, :], beta_slope[None, :], offset, owner, site, displaced)


def times(a, b, dims):
    return lax.dot_general(a, b, (dims, ((), ())), precision=HIGH, preferred_element_type=jnp.float32)


def plain(occupied, start, potential, perturbation, energy, beta, pair, in_plane):
    slabs = lax.axis_size("dom")
    bands, cells = start.shape
    depth = cells // PLANE
    total = cells * slabs
    whole = lax.all_gather(occupied, "band", axis=0, tiled=True)
    every = whole.shape[0]
    up = [(i, (i + 1) % slabs) for i in range(slabs)]
    down = [(j, i) for i, j in up]

    def local_part(field):
        before = lax.ppermute(field, "dom", up)
        after = lax.ppermute(field, "dom", down)
        grid = jnp.concatenate([before, field, after], axis=1)
        image = times(field.reshape(bands * depth, PLANE), in_plane, ((1,), (0,))).reshape(bands, cells)
        for d in range(1, 7):
            low = (depth - d) * PLANE
            high = (depth + d) * PLANE
            image += (-KINETIC * COEF[d]) * (grid[:, low : low + cells] + grid[:, high : high + cells])
        return image + (potential - energy) * field

    def correlate(field):
        return jnp.concatenate(
            [times(field, whole, ((1,), (1,))), times(field, beta, ((1,), (1,)))], axis=1
        )

    def operator(field, total_correlation):
        return (
            local_part(field)
            + (SHIFT / total) * times(total_correlation[:, :every], whole, ((1,), (0,)))
            + STRENGTH * times(total_correlation[:, every:], beta, ((1,), (0,)))
        )

    def dot(u, v):
        return jnp.sum(u * v, axis=1, keepdims=True)

    shaped = perturbation * occupied
    first, on_atoms, own, of_all = lax.psum(
        (
            times(shaped - SHIFT * start, whole, ((1,), (1,))),
            times(start, beta, ((1,), (1,))),
            times(occupied, pair, ((1,), (1,))),
            times(pair, whole, ((1,), (1,))),
        ),
        "dom",
    )
    own_radial, own_slope = own[:, 0:1], own[:, 1:2]
    first = first + STRENGTH * (own_radial * of_all[1:2] + own_slope * of_all[0:1])
    residual = (
        times(first * (1.0 / total), whole, ((1,), (0,)))
        - STRENGTH * times(on_atoms, beta, ((1,), (0,)))
        - local_part(start)
        - shaped
        - STRENGTH * (own_radial * pair[1:2] + own_slope * pair[0:1])
    )
    correlation, norm = lax.psum((correlate(residual), dot(residual, residual)), "dom")
    image = operator(residual, correlation)
    correlation, curve = lax.psum((correlate(image), dot(residual, image)), "dom")
    alpha = norm / curve
    again = operator(image, correlation)
    later = residual - alpha * image
    later_image = image - alpha * again
    new, bend, cross = lax.psum((dot(later, later), dot(later, later_image), dot(later, image)), "dom")
    ratio = new / norm
    step = new / (bend + ratio * (2.0 * cross + ratio * curve))
    answer = start + alpha * residual + step * (later + ratio * residual)
    return answer, later - step * (later_image + ratio * image)


NT = (((1,), (1,)), ((), ()))
NN = (((1,), (0,)), ((), ()))
MESH = pl.DeviceIdType.MESH


def parts_of(x):
    high = x.astype(jnp.bfloat16)
    return high, (x - high.astype(jnp.float32)).astype(jnp.bfloat16)


def product(a, b, dims):
    def one(u, v):
        return lax.dot_general(u, v, dims, preferred_element_type=jnp.float32)

    rows = a[0].shape[0]
    both = one(jnp.concatenate(a, axis=0), b[0])
    return both[:rows] + (one(a[0], b[1]) + both[rows:])


def fused_kernel(
    atoms,
    slabs,
    occ_in,
    start_in,
    pot_in,
    pert_in,
    energy_in,
    radial_in,
    slope_in,
    offset_in,
    owner_in,
    site_in,
    displaced,
    start,
    r0,
    w0,
    image,
    weights,
    occ,
    pot,
    pert,
    energy_row,
    radial,
    slope,
    offset,
    owner,
    site,
    energy,
    fields,
    plane_high,
    plane_low,
    whole,
    w_high,
    w_low,
    f_high,
    f_low,
    faces,
    part,
    pieces,
    summed,
    totals,
    last_part,
    last_in,
    band_send,
    band_recv,
    face_send,
    face_recv,
    hand_send,
    hand_recv,
    sum_send,
    sum_recv,
    all_send,
    all_recv,
    last_send,
    last_recv,
    local_sem,
):
    bands, cells = occ.shape
    every = 4 * bands
    total = cells * slabs
    band = lax.axis_index("band")
    slab = lax.axis_index("dom")
    sibling = band + 1 - 2 * (band % 2)
    across = (band + 2) % 4
    barrier = pltpu.get_barrier_semaphore()
    pl.semaphore_signal(barrier, inc=1, device_id={"band": sibling}, device_id_type=MESH)
    pl.semaphore_signal(barrier, inc=1, device_id={"band": across}, device_id_type=MESH)
    peers = [(slab + k) % slabs for k in range(slabs)]
    for k in range(1, slabs):
        pl.semaphore_signal(barrier, inc=1, device_id={"dom": peers[k]}, device_id_type=MESH)
    loads = [
        pltpu.make_async_copy(src, dst, local_sem.at[i])
        for i, (src, dst) in enumerate(
            (
                (offset_in, offset),
                (radial_in, radial),
                (slope_in, slope),
                (owner_in, owner),
                (site_in, site),
                (energy_in, energy_row),
                (pot_in, pot),
                (pert_in, pert),
                (start_in, start),
                (occ_in, occ),
            )
        )
    ]
    for load in loads:
        load.start()
    pl.semaphore_wait(barrier, slabs + 1)

    pending = []

    def send(src, dst, send_sem, recv_sem, device, begin=True):
        copy = pltpu.make_async_remote_copy(
            src_ref=src,
            dst_ref=dst,
            send_sem=send_sem,
            recv_sem=recv_sem,
            device_id=device,
            device_id_type=MESH,
        )
        if begin:
            copy.start()
        pending.append(copy)
        return copy

    chunk = bands // CHUNKS
    side = slab % 2
    beside = slab + 1 - 2 * side
    beyond = (slab + slabs + 2 - 4 * side) % slabs

    def send_face(turn, field, c, begin=True):
        return send(
            field.at[pl.ds(c * chunk, chunk)],
            faces.at[turn, side, pl.ds(c * chunk, chunk)],
            face_send.at[turn, c],
            face_recv.at[turn, c],
            {"dom": beside},
            begin,
        )

    def hand_over(turn, c):
        return send(
            faces.at[turn, 1 - side, pl.ds(c * chunk, chunk)],
            faces.at[turn, side, pl.ds(c * chunk, chunk)],
            hand_send.at[turn, c],
            hand_recv.at[turn, c],
            {"dom": beyond},
        )

    def hand_on(turn, copies, c):
        copies[c].wait_recv()
        copies.append(hand_over(turn, c))

    half = bands // PIECES
    crossing = [
        send(
            occ_in.at[pl.ds(c * half, half)],
            whole.at[1, pl.ds(c * half, half)],
            band_send.at[c],
            band_recv.at[c],
            {"band": across},
        )
        for c in range(PIECES)
    ]
    to_sibling = send(occ_in, whole.at[0], band_send.at[2 * PIECES], band_recv.at[2 * PIECES], {"band": sibling})
    moving = [send_face(0, start_in, c) for c in range(CHUNKS)]

    def hold(row, block):
        high, low = parts_of(block)
        w_high[row : row + block.shape[0], :] = high
        w_low[row : row + block.shape[0], :] = low

    def hold_field(block):
        high, low = parts_of(block)
        f_high[...] = high
        f_low[...] = low

    def plane_image(field, image, planes):
        for z in planes:
            cut = slice(z * PLANE, (z + 1) * PLANE)
            local_pot = jnp.concatenate(
                [pot[i : i + 1] for i in range(z * PLANE // 128, (z + 1) * PLANE // 128)], axis=1
            )
            image[:, cut] = product(
                (f_high[:, cut], f_low[:, cut]), (plane_high[...], plane_low[...]), NN
            ) + (local_pot - energy[:, 0:1]) * field[:, cut]

    def across_planes(turn, field, image, c):
        def group(i, carry):
            rows = pl.ds(pl.multiple_of(i * 8, 8), 8)
            grid = [
                ref[rows, z * PLANE : (z + 1) * PLANE]
                for ref in (faces.at[turn, 0], field, faces.at[turn, 1])
                for z in range(HALO)
            ]
            for z in range(HALO):
                cut = slice(z * PLANE, (z + 1) * PLANE)
                value = image[rows, cut]
                for d in range(1, 7):
                    value += (-KINETIC * COEF[d]) * (grid[HALO + z - d] + grid[HALO + z + d])
                image[rows, cut] = value
            return carry

        lax.fori_loop(c * chunk // 8, (c + 1) * chunk // 8, group, 0)

    def start_sum(turn):
        return [
            send(
                part.at[turn, pl.ds(pl.multiple_of(peers[k] * 8, 8), 8)],
                pieces.at[turn, k],
                sum_send.at[turn, k],
                sum_recv.at[turn, k],
                {"dom": peers[k]},
            )
            for k in range(1, slabs)
        ]

    def share_sum(turn, copies):
        mine = pl.ds(pl.multiple_of(slab * 8, 8), 8)
        value = part[turn, mine, :]
        for k in range(1, slabs):
            copies[k - 1].wait_recv()
            value += pieces[turn, k]
        summed[turn] = value
        shared = [
            send(
                summed.at[turn],
                totals.at[turn, mine],
                all_send.at[turn, k],
                all_recv.at[turn, k],
                {"dom": peers[k]},
            )
            for k in range(1, slabs)
        ]
        totals[turn, mine, :] = value
        return shared

    def finish_sum(shared):
        for copy in shared:
            copy.wait_recv()

    lane = lax.broadcasted_iota(jnp.int32, (bands, 128), 1)

    def correlate(rows):
        return product((f_high[...], f_low[...]), (w_high[rows, :], w_low[rows, :]), NT)

    def back(coefficients):
        return product(parts_of(coefficients), (w_high[...], w_low[...]), NN)

    pair = slice(every, every + 128)

    def pair_part(q, block):
        rows = slice(q * bands, (q + 2) * bands)
        both = product(
            (w_high[rows, :], w_low[rows, :]), (w_high[pair, :], w_low[pair, :]), NT
        )
        for i in range(2):
            mine = both[i * bands : (i + 1) * bands]
            if q + i:
                mine = pltpu.roll(mine, 2 * (q + i), 1)
            at = atoms + 2 * (q + i)
            block = jnp.where((lane == at) | (lane == at + 1), mine, block)
        return block

    one_cell = lax.broadcasted_iota(jnp.int32, (PLANE, PLANE), 0)
    other_cell = lax.broadcasted_iota(jnp.int32, (PLANE, PLANE), 1)
    along_x = (one_cell - other_cell) & (NX - 1)
    along_y = ((one_cell >> 4) - (other_cell >> 4)) & (NY - 1)
    away_x = jnp.minimum(along_x, NX - along_x)
    away_y = jnp.minimum(along_y, NY - along_y)
    away = jnp.where(away_x == 0, away_y, jnp.where(away_y == 0, away_x, NX))
    matrix = jnp.where(away == 0, -KINETIC * 3.0 * COEF[0], 0.0)
    for d in range(1, 7):
        matrix = jnp.where(away == d, -KINETIC * COEF[d], matrix)
    matrix_high, matrix_low = parts_of(matrix.astype(jnp.float32))
    plane_high[...] = matrix_high
    plane_low[...] = matrix_low

    for load in loads[:8]:
        load.wait()
    rows = lax.broadcasted_iota(jnp.int32, (bands, bands), 0)
    columns = lax.broadcasted_iota(jnp.int32, (bands, bands), 1)
    energy[...] = jnp.broadcast_to(
        jnp.sum(jnp.where(rows == columns, energy_row[...], 0.0), axis=1, keepdims=True), (bands, 128)
    )
    place_fields(
        slab, slabs, cells // PLANE, atoms, radial, slope, offset, owner, site, displaced, fields
    )
    for load in loads[8:]:
        load.wait()
    hold(0, occ[...])
    hold(every, fields[...])
    hold_field(start[...])
    plane_image(start, image, range(HALO))
    hand_on(0, moving, 0)
    hand_on(0, moving, 1)
    ends = slice(every, every + 128)
    on_start = correlate(ends)
    hand_on(0, moving, 2)
    shaped = pert[...] * occ[...]
    hold_field(shaped - SHIFT * start[...])
    to_sibling.wait_recv()
    hold(bands, whole[0])
    hand_on(0, moving, 3)
    part[0, :, 0 : 2 * bands] = correlate(slice(0, 2 * bands))
    on_fields = pair_part(0, on_start)
    passed = []
    for c in range(PIECES):
        crossing[c].wait_recv()
        passed.append(
            send(
                whole.at[1, pl.ds(c * half, half)],
                whole.at[2, pl.ds(c * half, half)],
                band_send.at[PIECES + c],
                band_recv.at[PIECES + c],
                {"band": sibling},
            )
        )
        hand_on(0, moving, 4 + c)
        hold(2 * bands + c * half, whole[1, c * half : (c + 1) * half])
        if c > 0:
            passed[c - 1].wait_recv()
            hold(3 * bands + (c - 1) * half, whole[2, (c - 1) * half : c * half])
    passed[PIECES - 1].wait_recv()
    hold(4 * bands - half, whole[2, bands - half :])
    part[0, :, 2 * bands : every] = correlate(slice(2 * bands, every))
    part[0, :, every:] = pair_part(2, on_fields)
    copies = start_sum(0)
    shared = share_sum(0, copies)
    for c in range(CHUNKS):
        moving[CHUNKS + c].wait_recv()
        across_planes(0, start, image, c)
    finish_sum(shared)
    last = totals[0, :, every:]
    own_radial, own_slope = last[:, atoms : atoms + 1], last[:, atoms + 1 : atoms + 2]
    swapped = jnp.where(
        lane == atoms, own_slope, jnp.where(lane == atoms + 1, own_radial, 0.0)
    )
    of_all = jnp.concatenate(
        [last] + [pltpu.roll(last, 128 - 2 * q, 1) for q in range(1, 4)], axis=0
    )
    first = totals[0, :, 0:every] + STRENGTH * product(parts_of(swapped), parts_of(of_all), NT)
    ends_part = jnp.where(lane < atoms, last, swapped)
    projected = back(jnp.concatenate([first * (1.0 / total), -STRENGTH * ends_part], axis=1))
    early = []
    for rows in (slice(0, 3 * chunk), slice(3 * chunk, bands)):
        r0[rows] = projected[rows] - image[rows] - pert[...] * occ[rows]
        if not early:
            early = [send_face(1, r0, c) for c in range(3)]

    def dot(u, v):
        return jnp.sum(u * v, axis=1, keepdims=True)

    def apply(turn, field, image, early, between=None):
        face = list(early)
        hold_field(field[...])
        on_all = correlate(slice(0, every + 128))
        part[turn, :, 0:every] = on_all[:, 0:every]
        part[turn, :, every:] = jnp.where(
            lane == atoms, dot(r0[...], field[...]), on_all[:, every:]
        )
        copies = start_sum(turn)
        face += [send_face(turn, field, c, False) for c in range(3, CHUNKS)]

        @pl.when(band % 2 == EAGER)
        def _():
            for copy in face[3:]:
                copy.start()

        @pl.when(band % 2 != EAGER)
        def _():
            for copy in face[3:DEPTH]:
                copy.start()

        plane_image(field, image, range(HALO))
        handed = []
        for c in range(CHUNKS):
            face[c].wait_recv()
            handed.append(hand_over(turn, c))
            if c + DEPTH < CHUNKS:

                @pl.when(band % 2 != EAGER)
                def _():
                    face[c + DEPTH].start()

            if c == SUM_AT:
                shared = share_sum(turn, copies)
            if c >= 4:
                handed[c - 4].wait_recv()
                across_planes(turn, field, image, c - 4)
        handed[CHUNKS - 4].wait_recv()
        across_planes(turn, field, image, CHUNKS - 4)
        finish_sum(shared)
        if between is not None:
            for c in range(CHUNKS - 3, CHUNKS):
                handed[c].wait_recv()
                across_planes(turn, field, image, c)
            between(totals[turn, :, every + atoms : every + atoms + 1])
        last = totals[turn, :, every:]
        coefficients = jnp.concatenate(
            [
                totals[turn, :, 0:every] * (SHIFT / total),
                jnp.where(lane < atoms, STRENGTH * last, 0.0),
            ],
            axis=1,
        )
        projected = back(coefficients)
        for rows in (slice(0, 3 * chunk), slice(3 * chunk, bands)):
            image[rows] += projected[rows]
            if between is None and not ahead:
                ahead.extend(send_face(turn + 1, image, c) for c in range(3))
        if between is None:
            for c in range(CHUNKS - 3, CHUNKS):
                handed[c].wait_recv()
                across_planes(turn, field, image, c)
        return last[:, atoms : atoms + 1], coefficients

    ahead = []
    norm, _ = apply(1, r0, w0, early)
    eye = jnp.where(
        lax.broadcasted_iota(jnp.int32, (128, 128), 0)
        == lax.broadcasted_iota(jnp.int32, (128, 128), 1),
        1.0,
        0.0,
    ).astype(jnp.float32)
    last_copies = []

    def send_scalars(curve):
        alpha = norm / curve
        later = r0[...] - alpha * w0[...]
        three = jnp.where(
            lane == 0,
            dot(later, later),
            jnp.where(
                lane == 1,
                dot(later, w0[...] - alpha * image[...]),
                jnp.where(lane == 2, dot(later, w0[...]), 0.0),
            ),
        )
        three = jnp.concatenate([three, jnp.zeros((128 - bands, 128), jnp.float32)], axis=0)
        last_part[...] = lax.dot_general(
            eye[0:8], three, NT, precision=HIGH, preferred_element_type=jnp.float32
        )
        last_copies.extend(
            send(last_part, last_in.at[k], last_send.at[k], last_recv.at[k], {"dom": peers[k]})
            for k in range(1, slabs)
        )

    curve, coefficients = apply(2, w0, image, ahead, send_scalars)
    alpha = norm / curve
    on_occupied = dot(totals[1] - alpha * totals[2], coefficients)
    value = last_part[...]
    for k in range(1, slabs):
        last_copies[k - 1].wait_recv()
        value += last_in[k]
    three = lax.dot_general(
        eye[0:bands], value, NT, precision=HIGH, preferred_element_type=jnp.float32
    )
    new, cross = three[:, 0:1], three[:, 2:3]
    bend = three[:, 1:2] - alpha * on_occupied
    ratio = new / norm
    step = new / (bend + ratio * (2.0 * cross + ratio * curve))
    weights[...] = jnp.where(
        lane == 0, alpha + step * (1.0 + ratio), jnp.where(lane == 1, step * alpha, 0.0)
    )
    for copy in pending:
        copy.wait_send()


def finish_kernel(start, r0, w0, z0, weights, answer, residual, held, sems):
    bands = start.shape[0]
    size = bands // FINISH
    copies = []
    for c in range(FINISH):
        rows = pl.ds(c * size, size)
        first, second = weights[rows, 0:1], weights[rows, 1:2]
        held[0, rows] = start[rows] + first * r0[rows] - second * w0[rows]
        held[1, rows] = r0[rows] - first * w0[rows] + second * z0[rows]
        for i, out in enumerate((answer, residual)):
            copy = pltpu.make_async_copy(held.at[i, rows], out.at[0, rows], sems.at[i, c])
            copy.start()
            copies.append(copy)
    for copy in copies:
        copy.wait()


def fused(
    occupied,
    start_guess,
    potential,
    perturbation,
    energy,
    beta_radial,
    beta_slope,
    offset,
    owner,
    site,
    displaced,
):
    slabs = lax.axis_size("dom")
    atoms = owner.shape[0]
    bands, cells = occupied.shape
    every = 4 * bands
    rows = every + 128
    f32, bf16, i32 = jnp.float32, jnp.bfloat16, jnp.int32
    vmem = pl.BlockSpec(memory_space=pltpu.VMEM)
    hbm = pl.BlockSpec(memory_space=pltpu.HBM)
    out = jax.ShapeDtypeStruct((bands, cells), f32)
    dma = pltpu.SemaphoreType.DMA
    points = offset.shape[1]
    state = pl.pallas_call(
        functools.partial(fused_kernel, atoms, slabs),
        out_shape=(out, out, out, out, jax.ShapeDtypeStruct((bands, 128), f32)),
        in_specs=[hbm] * 10 + [pl.BlockSpec(memory_space=pltpu.SMEM)],
        out_specs=(vmem,) * 5,
        scratch_shapes=[
            pltpu.VMEM((bands, cells), f32),
            pltpu.VMEM((cells // 128, 128), f32),
            pltpu.VMEM((1, cells), f32),
            pltpu.VMEM((1, bands), f32),
            pltpu.VMEM((1, points), f32),
            pltpu.VMEM((1, points), f32),
            pltpu.VMEM((3, points), i32),
            pltpu.VMEM((1, atoms), i32),
            pltpu.VMEM((3, atoms), i32),
            pltpu.VMEM((bands, 128), f32),
            pltpu.VMEM((128, cells), f32),
            pltpu.VMEM((PLANE, PLANE), bf16),
            pltpu.VMEM((PLANE, PLANE), bf16),
            pltpu.VMEM((3, bands, cells), f32),
            pltpu.VMEM((rows, cells), bf16),
            pltpu.VMEM((rows, cells), bf16),
            pltpu.VMEM((bands, cells), bf16),
            pltpu.VMEM((bands, cells), bf16),
            pltpu.VMEM((3, 2, bands, cells), f32),
            pltpu.VMEM((3, bands, rows), f32),
            pltpu.VMEM((3, slabs, 8, rows), f32),
            pltpu.VMEM((3, 8, rows), f32),
            pltpu.VMEM((3, bands, rows), f32),
            pltpu.VMEM((8, 128), f32),
            pltpu.VMEM((slabs, 8, 128), f32),
            dma((2 * PIECES + 1,)),
            dma((2 * PIECES + 1,)),
            dma((3, CHUNKS)),
            dma((3, CHUNKS)),
            dma((3, CHUNKS)),
            dma((3, CHUNKS)),
            dma((3, slabs)),
            dma((3, slabs)),
            dma((3, slabs)),
            dma((3, slabs)),
            dma((slabs,)),
            dma((slabs,)),
            dma((10,)),
        ],
        compiler_params=pltpu.CompilerParams(
            collective_id=0, has_side_effects=True, vmem_limit_bytes=40 * 1024 * 1024
        ),
    )(
        *(
            pltpu.with_memory_space_constraint(x, pltpu.HBM)
            for x in (
                occupied,
                start_guess[0],
                potential.reshape(cells // 128, 128),
                perturbation,
                energy[None, :],
                beta_radial[None, :],
                beta_slope[None, :],
                offset,
                owner[None, :],
                site,
            )
        ),
        displaced,
    )
    final = jax.ShapeDtypeStruct((1, bands, cells), f32)
    return pl.pallas_call(
        finish_kernel,
        out_shape=(final, final),
        in_specs=[vmem] * 5,
        out_specs=(hbm, hbm),
        scratch_shapes=[pltpu.VMEM((2, bands, cells), f32), dma((2, FINISH))],
        compiler_params=pltpu.CompilerParams(vmem_limit_bytes=16 * 1024 * 1024),
    )(*state)


def local(
    occupied,
    start_guess,
    potential,
    perturbation,
    band_energy,
    beta_radial,
    beta_slope,
    atom_owner,
    atom_site,
    sphere_offset,
    displaced,
):
    slabs = lax.axis_size("dom")
    bands, cells = start_guess.shape[1:]
    atoms = atom_owner.shape[0]
    fits = bands == 8 * slabs and lax.axis_size("band") == 4 and atoms % 16 == 0 and atoms <= 112
    if fits and cells == HALO * PLANE:
        return fused(
            occupied,
            start_guess,
            potential,
            perturbation,
            band_energy,
            beta_radial,
            beta_slope,
            sphere_offset,
            atom_owner,
            atom_site,
            displaced,
        )
    fields = atom_fields(
        slabs, cells, beta_radial, beta_slope, sphere_offset, atom_owner, atom_site, displaced
    )
    answer, residual = plain(
        occupied,
        start_guess[0],
        potential[None, :],
        perturbation,
        band_energy[:, None],
        fields[:atoms],
        fields[atoms : atoms + 8],
        jnp.asarray(plane_matrix()),
    )
    return answer[None], residual[None]


def solution(mesh):
    return jax.shard_map(
        local,
        mesh=mesh,
        in_specs=(
            P("band", "dom"),
            P(None, "band", "dom"),
            P("dom"),
            P(None, "dom"),
            P("band"),
            P(),
            P(),
            P(),
            P(),
            P(),
            P(),
        ),
        out_specs=(P(None, "band", "dom"), P(None, "band", "dom")),
        check_vma=False,
    )
```
